256 devices in a mesh: rad: 16 (over x, y_hi, core), fn: 16 (over y_lo, z).
Axes of the slice: x: 4, y: 4 (y_hi: 2, y_lo: 2; y = y_hi * 2 + y_lo), z: 8, core: 2. Of those that a mesh axis runs over, the one named last changes fastest.
Arguments:
- functions: bfloat16 [256, 640, 1202], P('fn', 'rad'), may hold values from -6 to 6
- orbital: float32 [640, 1202], P('rad'), may hold values from -6 to 6
- radial_weight: float32 [640], P('rad'), may hold values from 0.5 to 2
- ylm: bfloat16 [961, 1202], replicated, may hold values from -0.15625 to 0.15625
Outputs:
- potential: bfloat16 [256, 640, 1202], P('fn', 'rad')
- exchange_kernel: float32 [256, 256], P('rad', 'fn')
The draws below stay inside these ranges and needn't reach their ends.
All inputs are finite; a program needn't handle non-finite values.
Results may differ from the reference program's by a relative error of at most 0.0065.
Values may be sent and summed in bfloat16 or wider, within the bound.
A program may use at most 128 MiB of HBM per device.

```python
import math
import jax
import jax.numpy as jnp
import numpy as np
from jax import lax

ANGLES = 1202
LMAX = 30
FUNCS = 256
HARM = 961
RADII = 640


def block_scale(key, extent, cuts, smallest, largest):
    level, own = 1.0, jax.random.fold_in(key, 6)
    for dim, shards_of in cuts:
        steps = jnp.exp(jax.random.uniform(jax.random.fold_in(own, dim), (shards_of,), jnp.float32, smallest / len(cuts), largest / len(cuts)))
        level = level * jnp.repeat(steps, extent[dim] // shards_of).reshape([-1 if axis == dim else 1 for axis in range(len(extent))])
    return level


def noise(rng, dims, deviation, reach, split=(), held_as=jnp.bfloat16):
    level = block_scale(rng, dims, split, -0.22, 0.18) if split else 1.0
    drawn = jax.random.normal(rng, dims, jnp.float32) * deviation * level
    return jnp.minimum(jnp.maximum(drawn, -reach), reach).astype(held_as)


def setup_inputs(seed: int = 0) -> dict:
    seeds = jax.random.split(jax.random.key(seed), 5)
    return {
        "functions": noise(seeds[0], (FUNCS, RADII, ANGLES), 1.0, 6.0, ((0, 16), (1, 16))),
        "orbital": noise(seeds[1], (RADII, ANGLES), 1.0, 6.0, ((0, 16),), jnp.float32),
        "radial_weight": jnp.clip(jnp.exp(math.log(2.0) - 1.3862944 * jax.random.uniform(seeds[2], (RADII,), jnp.float32) ** block_scale(seeds[2], (RADII,), ((0, 16),), -0.2, 0.2)), 0.5, 2.0),
        "ylm": noise(seeds[3], (HARM, ANGLES), ANGLES ** -0.5, 0.15625),
    }


def degrees():
    table = np.repeat(np.arange(LMAX + 1), 2 * np.arange(LMAX + 1) + 1)
    return jnp.asarray(table, jnp.float32)


def local_green(weighted, radius, degree):
    count = radius.shape[0]
    source = weighted.astype(jnp.float32) / radius[None, :, None]
    logr = jnp.log(radius)[:, None]
    grow = jnp.exp((degree[None, :] + 1.0) * logr)
    shrink = jnp.exp(-degree[None, :] * logr)
    rows = jnp.arange(count, dtype=jnp.int32)
    lower = (rows[None, :] <= rows[:, None]).astype(jnp.float32)
    upper = (rows[None, :] >= rows[:, None]).astype(jnp.float32)
    grown = source * grow[None]
    shrunk = source * shrink[None]
    out_sum = jnp.einsum("ij,fjm->fim", lower, grown, precision=lax.Precision.HIGHEST)
    in_sum = jnp.einsum("ij,fjm->fim", upper, shrunk, precision=lax.Precision.HIGHEST)
    return out_sum, in_sum, source, grow, shrink, grown, shrunk


def reference(functions, orbital, radial_weight, ylm):
    spacing = 3.0 / RADII
    radius = 1.0 + spacing * (jnp.arange(RADII).astype(jnp.float32) + 0.5)
    quadrature = spacing * radial_weight * radius * radius
    degree = degrees()
    multipole = 4.0 * math.pi / (2.0 * degree + 1.0)

    def one_block(block):
        density = (orbital[None] * block).astype(jnp.bfloat16)
        projected = lax.dot_general(density, ylm, (((2,), (1,)), ((), ())), preferred_element_type=jnp.float32)
        weighted = (projected * quadrature[None, :, None]).astype(jnp.bfloat16)
        out_sum, in_sum, source, grow, shrink, grown, shrunk = local_green(weighted, radius, degree)
        outward = out_sum / grow[None]
        inward = in_sum / shrink[None]
        coefficients = (multipole * (outward + inward - source)).astype(jnp.bfloat16)
        potential = lax.dot_general(coefficients, ylm, (((2,), (0,)), ((), ())), preferred_element_type=jnp.float32).astype(jnp.bfloat16)
        return potential, weighted, coefficients

    blocks = functions.reshape(FUNCS // 16, 16, RADII, ANGLES)
    potential, weighted, coefficients = lax.map(one_block, blocks)
    potential = potential.reshape(FUNCS, RADII, ANGLES)
    weighted = weighted.reshape(FUNCS, -1)
    coefficients = coefficients.reshape(FUNCS, -1)
    kernel = lax.dot_general(weighted, coefficients, (((1,), (1,)), ((), ())), preferred_element_type=jnp.float32)
    kernel = kernel * (4.0 * math.pi / ANGLES)
    return potential, kernel
```

```python
import functools
import math

import jax
import jax.numpy as jnp
from jax import lax
from jax.experimental import pallas as pl
from jax.experimental.pallas import tpu as pltpu
from jax.sharding import PartitionSpec as P

MESH = pl.DeviceIdType.MESH
F32, BF16 = jnp.float32, jnp.bfloat16
ANGLES, HARM, RADII = 1202, 961, 640
RADS, FNS = 16, 16
ROWS, FUNCS = 40, 16
SPACING = 3.0 / RADII
CHUNKS, WIDE = 4, 256
TILES = 2 * ROWS // FNS
FN_STEPS = [(y, z) for z in (4, 3, 5, 2, 6, 1, 7, 0) for y in (0, 1) if (y, z) != (0, 0)]


def degree_of(first, width):
    m = first + lax.broadcasted_iota(jnp.int32, (1, width), 1)
    return jnp.floor(jnp.sqrt(m.astype(F32) + 0.5))


def kernel(
    functions, orbital, weight, ylm,
    potential, matrix,
    fn_v, orb_v, ylm_v, dens, proj, src, inw, coef, pot_v,
    decay, rise, scale, fall, couple_o, couple_n,
    y_buf, y_in, x_buf, x_in, edge, edge_in, gram, part_in, slab, slab_in,
    load_sem, store_sem, y_send, y_recv, x_send, x_recv, e_send, e_recv, p_send, p_recv, s_send, s_recv,
):
    rad, fn = lax.axis_index("rad"), lax.axis_index("fn")
    fn_y, fn_z = fn // 8, lax.rem(fn, 8)
    fn_peers = [lax.rem(fn_y + y, 2) * 8 + lax.rem(fn_z + z, 8) for y, z in FN_STEPS]

    loads = [
        pltpu.make_async_copy(functions, fn_v, load_sem.at[0]),
        pltpu.make_async_copy(orbital, orb_v, load_sem.at[1]),
        pltpu.make_async_copy(ylm, ylm_v, load_sem.at[2]),
    ]
    for copy in loads:
        copy.start()

    barrier = pltpu.get_barrier_semaphore()
    for peer in fn_peers:
        pl.semaphore_signal(barrier, inc=1, device_id=(rad, peer), device_id_type=MESH)

    @pl.loop(1, RADS)
    def _(step):
        pl.semaphore_signal(barrier, inc=1, device_id=(lax.rem(rad + step, RADS), fn), device_id_type=MESH)

    def radius_of(position):
        return 1.0 + SPACING * (position.astype(F32) + 0.5)

    def minus_log(x):
        return x * (1.0 + x * (0.5 + x * (1.0 / 3.0 + x * 0.25)))

    rows = lax.broadcasted_iota(jnp.int32, (ROWS, 1), 0)
    radius = radius_of(rad * ROWS + rows)
    gap = SPACING / radius
    step_log = minus_log(gap)
    next_log = minus_log(SPACING / radius_of(rad * ROWS + rows + 1))
    for c in range(CHUNKS):
        lanes = pl.ds(c * WIDE, WIDE)
        deg = degree_of(c * WIDE, WIDE)
        decay[:, lanes] = jnp.exp(-deg * next_log)
        rise[:, lanes] = jnp.exp(-deg * step_log) * (1.0 - gap)
        t = (2.0 * deg + 1.0) * step_log
        em = t * (1.0 - t * (1 / 2) * (1.0 - t * (1 / 3) * (1.0 - t * (1 / 4) * (1.0 - t * (1 / 5) * (1.0 - t * (1 / 6) * (1.0 - t * (1 / 7)))))))
        em = jnp.where(rows == 0, 1.0, em)
        scale[:, lanes] = jnp.sqrt((16.0 * math.pi**2 / ANGLES) / (2.0 * deg + 1.0) * radius * em)

    for copy in loads[:2]:
        copy.wait()
    orb = orb_v[...]

    @pl.loop(0, FUNCS // 2)
    def _(pair):
        d = fn_v[pl.ds(2 * pair, 2)].astype(F32) * orb[None]
        dens[pl.ds(pl.multiple_of(pair * 80, 16), 80), :] = d.reshape(80, ANGLES).astype(BF16)

    loads[2].wait()

    for c in range(CHUNKS):
        width = min(WIDE, HARM - c * WIDE)
        out = lax.dot_general(
            dens[...], ylm_v[c * WIDE:c * WIDE + width, :], (((1,), (1,)), ((), ())), preferred_element_type=F32
        )
        if width == WIDE:
            proj[0] = out[:, :128]
            proj[1] = out[:, 128:]
        else:
            proj[0] = out[:, :128]
            proj[1] = jnp.zeros_like(proj[1])
            proj[1, :, 0:width - 128] = out[:, 128:]

        base = c * WIDE

        def back(step, n):
            first_row = pl.multiple_of(8 * (ROWS // 8 - 1 - step), 8)
            down = decay[pl.ds(first_row, 8), base:base + WIDE]
            up = scale[pl.ds(first_row, 8), base:base + WIDE]
            for k in reversed(range(8)):
                i = first_row + k
                r_i = 1.0 + SPACING * ((rad * ROWS + i).astype(F32) + 0.5)
                factor = SPACING * weight[i] * r_i
                new = []
                for h in range(2):
                    lanes = slice(128 * h, 128 * h + 128)
                    s = proj[h, pl.ds(i, FUNCS, stride=ROWS), :] * factor
                    src[2 * c + h, i] = s
                    v = s + down[k:k + 1, lanes] * n[h]
                    inw[2 * c + h, i] = v
                    y_buf[c, 2 * i + h] = (v * up[k:k + 1, lanes]).astype(BF16)
                    new.append(v)
                n = tuple(new)
            return n

        zero = jnp.zeros((FUNCS, 128), F32)
        first = lax.fori_loop(0, ROWS // 8, back, (zero, zero))
        for h in range(2):
            edge[1, :, base + 128 * h:base + 128 * h + 128] = first[h].astype(BF16)

        if c == 0:
            pl.semaphore_wait(barrier, len(FN_STEPS) + RADS - 1)
        for peer in fn_peers:
            pltpu.make_async_remote_copy(
                src_ref=y_buf.at[c, pl.ds(peer * TILES, TILES)],
                dst_ref=y_in.at[c, fn],
                send_sem=y_send.at[c, peer],
                recv_sem=y_recv.at[c, fn],
                device_id=(rad, peer),
                device_id_type=MESH,
            ).start()
        y_in[c, fn] = y_buf[c, pl.ds(fn * TILES, TILES)]

        def forth(step, o):
            first_row = pl.multiple_of(8 * step, 8)
            up = rise[pl.ds(first_row, 8), base:base + WIDE]
            for k in range(8):
                o = tuple(
                    src[2 * c + h, first_row + k] + up[k:k + 1, 128 * h:128 * h + 128] * o[h] for h in range(2)
                )
            return o

        last = lax.fori_loop(0, ROWS // 8, forth, (zero, zero))
        for h in range(2):
            edge[0, :, base + 128 * h:base + 128 * h + 128] = last[h].astype(BF16)

    @pl.loop(1, RADS)
    def _(step):
        peer = lax.rem(rad + step, RADS)
        pltpu.make_async_remote_copy(
            src_ref=edge.at[jnp.where(peer > rad, 0, 1)],
            dst_ref=edge_in.at[rad],
            send_sem=e_send.at[peer],
            recv_sem=e_recv.at[rad],
            device_id=(peer, fn),
            device_id_type=MESH,
        ).start()

    edge_in[rad] = jnp.zeros((FUNCS, CHUNKS * WIDE), BF16)
    blocks = lax.broadcasted_iota(jnp.int32, (RADS, 1), 0)
    log_last = jnp.log(radius_of(blocks * ROWS + (ROWS - 1)))
    log_first = jnp.log(radius_of(blocks * ROWS))
    spot = jnp.full((1, 1), rad, jnp.int32)
    log_end = jnp.log(radius_of(spot * ROWS - 1))
    log_next = jnp.log(radius_of(spot * ROWS + ROWS))
    log_row = jnp.log(radius)
    for c in range(CHUNKS):
        lanes = pl.ds(c * WIDE, WIDE)
        deg = degree_of(c * WIDE, WIDE)
        couple_o[:, lanes] = jnp.where(blocks < spot, jnp.exp((deg + 1.0) * jnp.minimum(log_last - log_end, 0.0)), 0.0)
        couple_n[:, lanes] = jnp.where(blocks > spot, jnp.exp(deg * jnp.minimum(log_next - log_first, 0.0)), 0.0)
        fall[:, lanes] = jnp.exp(deg * jnp.minimum(log_row - log_next, 0.0))

    @pl.loop(1, RADS)
    def _(step):
        peer = lax.rem(rad + step, RADS)
        pltpu.make_async_remote_copy(
            src_ref=edge.at[0], dst_ref=edge_in.at[peer], send_sem=e_send.at[peer], recv_sem=e_recv.at[peer],
            device_id=(peer, fn), device_id_type=MESH,
        ).wait_recv()

    lane = lax.broadcasted_iota(jnp.int32, (FUNCS, 128), 1)
    for t in range(2 * CHUNKS):
        lanes = slice(128 * t, 128 * t + 128)
        out_carry = jnp.zeros((FUNCS, 128), F32)
        in_carry = jnp.zeros((FUNCS, 128), F32)
        for b in range(RADS):
            e = edge_in[b, :, lanes].astype(F32)
            out_carry = out_carry + couple_o[b:b + 1, lanes] * e
            in_carry = in_carry + couple_n[b:b + 1, lanes] * e
        a_tile = inw[t, 0] * scale[0:1, lanes]
        p_tile = out_carry * (scale[0:1, lanes] * rise[0:1, lanes])
        x_buf[2 * t] = jnp.where(lane < 64, a_tile, pltpu.roll(p_tile, 64, 1)).astype(BF16)
        x_buf[2 * t + 1] = jnp.where(lane < 64, pltpu.roll(a_tile, 64, 1), p_tile).astype(BF16)
        multipole = (4.0 * math.pi) / (2.0 * degree_of(128 * t, 128) + 1.0)

        def forth(step, o):
            first_row = pl.multiple_of(8 * step, 8)
            up = rise[pl.ds(first_row, 8), lanes]
            far = fall[pl.ds(first_row, 8), lanes]
            for k in range(8):
                i = first_row + k
                grown = up[k:k + 1] * o
                total = grown + inw[t, i] + far[k:k + 1] * in_carry
                coef[t, pl.ds(i, FUNCS, stride=ROWS), :] = multipole * total
                o = grown + src[t, i]
            return o

        lax.fori_loop(0, ROWS // 8, forth, out_carry)

    for peer in fn_peers:
        pltpu.make_async_remote_copy(
            src_ref=x_buf.at[peer], dst_ref=x_in.at[fn], send_sem=x_send.at[peer], recv_sem=x_recv.at[fn],
            device_id=(rad, peer), device_id_type=MESH,
        ).start()
    x_in[fn] = x_buf[fn]

    @pl.loop(0, FUNCS // 4)
    def _(quad):
        at = pl.ds(pl.multiple_of(quad * 160, 16), 160)
        left = jnp.concatenate([coef[t, at, :].astype(BF16) for t in range(2 * CHUNKS)], axis=1)[:, :HARM]
        out = jnp.dot(left, ylm_v[...], preferred_element_type=F32)
        pot_v[pl.ds(4 * quad, 4)] = out.reshape(4, ROWS, ANGLES).astype(BF16)

    store = pltpu.make_async_copy(pot_v, potential, store_sem)
    store.start()

    def gram_of(left, right):
        return lax.dot_general(left, right, (((1,), (1,)), ((), ())), preferred_element_type=F32)

    for c in range(CHUNKS):
        for peer in fn_peers:
            pltpu.make_async_remote_copy(
                src_ref=y_buf.at[c, pl.ds(0, TILES)], dst_ref=y_in.at[c, peer], send_sem=y_send.at[c, peer],
                recv_sem=y_recv.at[c, peer], device_id=(rad, peer), device_id_type=MESH,
            ).wait_recv()
        x = jnp.concatenate([y_in[c, :, t].reshape(FNS * FUNCS, 128) for t in range(TILES)], axis=1)
        if c == 0:
            gram[...] = gram_of(x, x)
        else:
            gram[...] += gram_of(x, x)

    for peer in fn_peers:
        pltpu.make_async_remote_copy(
            src_ref=x_buf.at[peer], dst_ref=x_in.at[peer], send_sem=x_send.at[peer], recv_sem=x_recv.at[peer],
            device_id=(rad, peer), device_id_type=MESH,
        ).wait_recv()
    x = x_in[...].reshape(FNS * FUNCS, 128)
    gram[...] += gram_of(x, jnp.concatenate([x[:, 64:], x[:, :64]], axis=1))

    def part_copy(peer, slot):
        return pltpu.make_async_remote_copy(
            src_ref=gram.at[pl.ds(pl.multiple_of(peer * FUNCS, 8), FUNCS)], dst_ref=part_in.at[slot],
            send_sem=p_send.at[peer], recv_sem=p_recv.at[slot], device_id=(peer, fn), device_id_type=MESH,
        )

    @pl.loop(1, RADS)
    def _(step):
        part_copy(lax.rem(rad + step, RADS), rad).start()

    part_in[rad] = gram[pl.ds(pl.multiple_of(rad * FUNCS, 8), FUNCS), :]

    @pl.loop(1, RADS)
    def _(step):
        peer = lax.rem(rad + step, RADS)
        part_copy(peer, peer).wait_recv()

    total = part_in[0]
    for b in range(1, RADS):
        total = total + part_in[b]
    slab[0] = total[:, :128]
    slab[1] = total[:, 128:]

    def slab_copy(peer, slot):
        return pltpu.make_async_remote_copy(
            src_ref=slab.at[peer // 8], dst_ref=slab_in.at[slot], send_sem=s_send.at[peer],
            recv_sem=s_recv.at[slot], device_id=(rad, peer), device_id_type=MESH,
        )

    for peer in fn_peers:
        slab_copy(peer, fn).start()
    slab_in[fn] = slab[fn // 8]
    for peer in fn_peers:
        slab_copy(peer, peer).wait_recv()
    total = slab_in[0]
    for b in range(1, FNS):
        total = total + slab_in[b]
    shift = lax.rem(128 - 16 * lax.rem(fn, 8), 128)
    matrix[...] = pltpu.roll(total, shift, 1)[:, :FUNCS]

    for peer in fn_peers:
        for c in range(CHUNKS):
            pltpu.make_async_remote_copy(
                src_ref=y_buf.at[c, pl.ds(peer * TILES, TILES)], dst_ref=y_in.at[c, fn], send_sem=y_send.at[c, peer],
                recv_sem=y_recv.at[c, fn], device_id=(rad, peer), device_id_type=MESH,
            ).wait_send()
        pltpu.make_async_remote_copy(
            src_ref=x_buf.at[peer], dst_ref=x_in.at[fn], send_sem=x_send.at[peer], recv_sem=x_recv.at[fn],
            device_id=(rad, peer), device_id_type=MESH,
        ).wait_send()
        slab_copy(peer, fn).wait_send()

    @pl.loop(1, RADS)
    def _(step):
        peer = lax.rem(rad + step, RADS)
        pltpu.make_async_remote_copy(
            src_ref=edge.at[0], dst_ref=edge_in.at[rad], send_sem=e_send.at[peer], recv_sem=e_recv.at[rad],
            device_id=(peer, fn), device_id_type=MESH,
        ).wait_send()
        part_copy(peer, rad).wait_send()

    store.wait()


def local(functions, orbital, radial_weight, ylm):
    any_ = pl.BlockSpec(memory_space=pl.ANY)
    vmem, dma = pltpu.VMEM, pltpu.SemaphoreType.DMA
    lanes = CHUNKS * WIDE
    return pl.pallas_call(
        kernel,
        out_shape=(
            jax.ShapeDtypeStruct((FUNCS, ROWS, ANGLES), BF16),
            jax.ShapeDtypeStruct((FUNCS, FUNCS), F32),
        ),
        in_specs=[any_, any_, pl.BlockSpec(memory_space=pltpu.SMEM), any_],
        out_specs=(any_, pl.BlockSpec(memory_space=pltpu.VMEM)),
        scratch_shapes=[
            vmem((FUNCS, ROWS, ANGLES), BF16),
            vmem((ROWS, ANGLES), F32),
            vmem((HARM, ANGLES), BF16),
            vmem((FUNCS * ROWS, ANGLES), BF16),
            vmem((2, FUNCS * ROWS, 128), F32),
            vmem((2 * CHUNKS, ROWS, FUNCS, 128), F32),
            vmem((2 * CHUNKS, ROWS, FUNCS, 128), F32),
            vmem((2 * CHUNKS, FUNCS * ROWS, 128), F32),
            vmem((FUNCS, ROWS, ANGLES), BF16),
            vmem((ROWS, lanes), F32),
            vmem((ROWS, lanes), F32),
            vmem((ROWS, lanes), F32),
            vmem((ROWS, lanes), F32),
            vmem((RADS, lanes), F32),
            vmem((RADS, lanes), F32),
            vmem((CHUNKS, 2 * ROWS, FUNCS, 128), BF16),
            vmem((CHUNKS, FNS, TILES, FUNCS, 128), BF16),
            vmem((FNS, FUNCS, 128), BF16),
            vmem((FNS, FUNCS, 128), BF16),
            vmem((2, FUNCS, lanes), BF16),
            vmem((RADS, FUNCS, lanes), BF16),
            vmem((FNS * FUNCS, FNS * FUNCS), F32),
            vmem((RADS, FUNCS, FNS * FUNCS), F32),
            vmem((2, FUNCS, 128), F32),
            vmem((FNS, FUNCS, 128), F32),
            dma((3,)), dma(()),
            dma((CHUNKS, FNS)), dma((CHUNKS, FNS)),
            dma((FNS,)), dma((FNS,)),
            dma((RADS,)), dma((RADS,)),
            dma((RADS,)), dma((RADS,)),
            dma((FNS,)), dma((FNS,)),
        ],
        compiler_params=pltpu.CompilerParams(
            collective_id=0, has_side_effects=True, vmem_limit_bytes=48 * 2**20
        ),
    )(functions, orbital, radial_weight, ylm)


def solution(mesh):
    in_specs = (P("fn", "rad", None), P("rad", None), P("rad"), P())
    out_specs = (P("fn", "rad", None), P("rad", "fn"))
    return jax.shard_map(local, mesh=mesh, in_specs=in_specs, out_specs=out_specs, check_vma=False)
```

```python
import functools
import math

import jax
import jax.numpy as jnp
from jax import lax
from jax.experimental import pallas as pl
from jax.experimental.pallas import tpu as pltpu
from jax.sharding import PartitionSpec as P

MESH = pl.DeviceIdType.MESH
F32, BF16 = jnp.float32, jnp.bfloat16
ANGLES, HARM, RADII = 1202, 961, 640
RADS, FNS = 16, 16
ROWS, FUNCS = 40, 16
SPACING = 3.0 / RADII
CHUNKS, WIDE = 4, 256
TILES = (5, 5, 5, 4)
FN_STEPS = [(y, z) for z in (4, 3, 5, 2, 6, 1, 7, 0) for y in (0, 1) if (y, z) != (0, 0)]


def degree_of(first, width):
    m = first + lax.broadcasted_iota(jnp.int32, (1, width), 1)
    return jnp.floor(jnp.sqrt(m.astype(F32) + 0.5))


def swap_blocks(x):
    row = lax.broadcasted_iota(jnp.int32, (8, 128), 0)
    block = lax.broadcasted_iota(jnp.int32, (8, 128), 1) // 16
    for b in (1, 2, 4):
        row_bit, block_bit = (row // b) % 2, (block // b) % 2
        above = pltpu.roll(pltpu.roll(x, 8 - b, 0), 16 * b, 1)
        below = pltpu.roll(pltpu.roll(x, b, 0), 128 - 16 * b, 1)
        x = jnp.where(row_bit == block_bit, x, jnp.where(block_bit == 1, above, below))
    return x


def kernel(
    functions, orbital, weight, ylm,
    potential, matrix,
    fn_v, orb_v, ylm_v, dens, proj, src, inw, coef,
    decay, rise, scale, fall, couple_o, couple_n,
    y_buf, y_in, x_buf, x_in, edge, edge_in, gram, part, part_in, slab, slab_in,
    load_sem, y_send, y_recv, x_send, x_recv, e_send, e_recv, p_send, p_recv, s_send, s_recv,
):
    rad, fn = lax.axis_index("rad"), lax.axis_index("fn")
    fn_y, fn_z = fn // 8, lax.rem(fn, 8)
    fn_peers = [lax.rem(fn_y + y, 2) * 8 + lax.rem(fn_z + z, 8) for y, z in FN_STEPS]

    loads = [
        pltpu.make_async_copy(functions, fn_v, load_sem.at[0]),
        pltpu.make_async_copy(orbital, orb_v, load_sem.at[1]),
        pltpu.make_async_copy(ylm, ylm_v, load_sem.at[2]),
    ]
    for copy in loads:
        copy.start()

    barrier = pltpu.get_barrier_semaphore()
    for peer in fn_peers:
        pl.semaphore_signal(barrier, inc=1, device_id=(rad, peer), device_id_type=MESH)

    @pl.loop(1, RADS)
    def _(step):
        pl.semaphore_signal(barrier, inc=1, device_id=(lax.rem(rad + step, RADS), fn), device_id_type=MESH)

    def y_copy(c, peer, slot):
        return pltpu.make_async_remote_copy(
            src_ref=y_buf.at[c, pl.ds(peer * TILES[c], TILES[c])], dst_ref=y_in.at[c, slot, pl.ds(0, TILES[c])],
            send_sem=y_send.at[c, peer], recv_sem=y_recv.at[c, slot], device_id=(rad, peer), device_id_type=MESH,
        )

    def radius_of(position):
        return 1.0 + SPACING * (position.astype(F32) + 0.5)

    def minus_log(x):
        return x * (1.0 + x * (0.5 + x * (1.0 / 3.0 + x * 0.25)))

    rows = lax.broadcasted_iota(jnp.int32, (ROWS, 1), 0)
    radius = radius_of(rad * ROWS + rows)
    gap = SPACING / radius
    step_log = minus_log(gap)
    next_log = minus_log(SPACING / radius_of(rad * ROWS + rows + 1))
    for c in range(CHUNKS):
        lanes = pl.ds(c * WIDE, WIDE)
        deg = degree_of(c * WIDE, WIDE)
        decay[:, lanes] = jnp.exp(-deg * next_log)
        rise[:, lanes] = jnp.exp(-deg * step_log) * (1.0 - gap)
        t = (2.0 * deg + 1.0) * step_log
        em = t * (1.0 - t * (1 / 2) * (1.0 - t * (1 / 3) * (1.0 - t * (1 / 4) * (1.0 - t * (1 / 5) * (1.0 - t * (1 / 6) * (1.0 - t * (1 / 7)))))))
        em = jnp.where(rows == 0, 1.0, em)
        scale[:, lanes] = jnp.sqrt((16.0 * math.pi**2 / ANGLES) / (2.0 * deg + 1.0) * radius * em)

    for copy in loads[:2]:
        copy.wait()
    orb = orb_v[...]

    @pl.loop(0, FUNCS // 2)
    def _(pair):
        d = fn_v[pl.ds(2 * pair, 2)].astype(F32) * orb[None]
        dens[pl.ds(pl.multiple_of(pair * 80, 16), 80), :] = d.reshape(80, ANGLES).astype(BF16)

    loads[2].wait()

    lane = lax.broadcasted_iota(jnp.int32, (FUNCS, 128), 1)
    for c in range(CHUNKS):
        width = min(WIDE, HARM - c * WIDE)
        out = lax.dot_general(
            dens[...], ylm_v[:, c * WIDE:c * WIDE + width], (((1,), (0,)), ((), ())), preferred_element_type=F32
        )
        if width == WIDE:
            proj[0] = out[:, :128]
            proj[1] = out[:, 128:]
        else:
            proj[0] = out[:, :128]
            proj[1] = jnp.zeros_like(proj[1])
            proj[1, :, 0:width - 128] = out[:, 128:]

        base = c * WIDE

        def back(step, carry):
            n, spare = carry
            first_row = pl.multiple_of(8 * (ROWS // 8 - 1 - step), 8)
            down = decay[pl.ds(first_row, 8), base:base + WIDE]
            up = scale[pl.ds(first_row, 8), base:base + WIDE]
            for k in reversed(range(8)):
                i = first_row + k
                r_i = 1.0 + SPACING * ((rad * ROWS + i).astype(F32) + 0.5)
                factor = SPACING * weight[i] * r_i
                new = []
                for h in range(2):
                    lanes = slice(128 * h, 128 * h + 128)
                    s = proj[h, pl.ds(i, FUNCS, stride=ROWS), :] * factor
                    src[2 * c + h, i] = s
                    v = s + down[k:k + 1, lanes] * n[h]
                    inw[2 * c + h, i] = v
                    y = v * up[k:k + 1, lanes]
                    if width == WIDE:
                        y_buf[c, 2 * i + h] = y.astype(BF16)
                    elif h == 0:
                        y_buf[c, i] = y.astype(BF16)
                    else:
                        spare = jnp.where(lane == i, y[:, 64:65], spare)
                        if k % 2:
                            odd = pltpu.roll(y, 64, 1)
                        else:
                            y_buf[c, ROWS + first_row // 2 + k // 2] = jnp.where(lane < 64, y, odd).astype(BF16)
                    new.append(v)
                n = tuple(new)
            return n, spare

        zero = jnp.zeros((FUNCS, 128), F32)
        first, spare = lax.fori_loop(0, ROWS // 8, back, ((zero, zero), zero))
        if width < WIDE:
            y_buf[c, ROWS + ROWS // 2] = spare.astype(BF16)
            y_buf[c, ROWS + ROWS // 2 + 1:FNS * TILES[c]] = jnp.zeros((3, FUNCS, 128), BF16)
        for h in range(2):
            edge[1, :, base + 128 * h:base + 128 * h + 128] = first[h].astype(BF16)

        if c == 0:
            pl.semaphore_wait(barrier, len(FN_STEPS) + RADS - 1)
        for peer in fn_peers:
            y_copy(c, peer, fn).start()
        y_in[c, fn, 0:TILES[c]] = y_buf[c, pl.ds(fn * TILES[c], TILES[c])]

        def forth(step, o):
            first_row = pl.multiple_of(8 * step, 8)
            up = rise[pl.ds(first_row, 8), base:base + WIDE]
            for k in range(8):
                o = tuple(
                    src[2 * c + h, first_row + k] + up[k:k + 1, 128 * h:128 * h + 128] * o[h] for h in range(2)
                )
            return o

        last = lax.fori_loop(0, ROWS // 8, forth, (zero, zero))
        for h in range(2):
            edge[0, :, base + 128 * h:base + 128 * h + 128] = last[h].astype(BF16)

    @pl.loop(1, RADS)
    def _(step):
        peer = lax.rem(rad + step, RADS)
        pltpu.make_async_remote_copy(
            src_ref=edge.at[jnp.where(peer > rad, 0, 1)],
            dst_ref=edge_in.at[rad],
            send_sem=e_send.at[peer],
            recv_sem=e_recv.at[rad],
            device_id=(peer, fn),
            device_id_type=MESH,
        ).start()

    edge_in[rad] = jnp.zeros((FUNCS, CHUNKS * WIDE), BF16)
    blocks = lax.broadcasted_iota(jnp.int32, (RADS, 1), 0)
    log_last = jnp.log(radius_of(blocks * ROWS + (ROWS - 1)))
    log_first = jnp.log(radius_of(blocks * ROWS))
    spot = jnp.full((1, 1), rad, jnp.int32)
    log_end = jnp.log(radius_of(spot * ROWS - 1))
    log_next = jnp.log(radius_of(spot * ROWS + ROWS))
    log_row = jnp.log(radius)
    for c in range(CHUNKS):
        lanes = pl.ds(c * WIDE, WIDE)
        deg = degree_of(c * WIDE, WIDE)
        couple_o[:, lanes] = jnp.where(blocks < spot, jnp.exp((deg + 1.0) * jnp.minimum(log_last - log_end, 0.0)), 0.0)
        couple_n[:, lanes] = jnp.where(blocks > spot, jnp.exp(deg * jnp.minimum(log_next - log_first, 0.0)), 0.0)
        fall[:, lanes] = jnp.exp(deg * jnp.minimum(log_row - log_next, 0.0))

    @pl.loop(1, RADS)
    def _(step):
        peer = lax.rem(rad + step, RADS)
        pltpu.make_async_remote_copy(
            src_ref=edge.at[0], dst_ref=edge_in.at[peer], send_sem=e_send.at[peer], recv_sem=e_recv.at[peer],
            device_id=(peer, fn), device_id_type=MESH,
        ).wait_recv()

    for t in range(2 * CHUNKS):
        lanes = slice(128 * t, 128 * t + 128)
        out_carry = jnp.zeros((FUNCS, 128), F32)
        in_carry = jnp.zeros((FUNCS, 128), F32)
        for b in range(RADS):
            e = edge_in[b, :, lanes].astype(F32)
            out_carry = out_carry + couple_o[b:b + 1, lanes] * e
            in_carry = in_carry + couple_n[b:b + 1, lanes] * e
        a_tile = inw[t, 0] * scale[0:1, lanes]
        p_tile = out_carry * (scale[0:1, lanes] * rise[0:1, lanes])
        x_buf[2 * t] = jnp.where(lane < 64, a_tile, pltpu.roll(p_tile, 64, 1)).astype(BF16)
        x_buf[2 * t + 1] = jnp.where(lane < 64, pltpu.roll(a_tile, 64, 1), p_tile).astype(BF16)
        multipole = (4.0 * math.pi) / (2.0 * degree_of(128 * t, 128) + 1.0)

        def forth(step, o):
            first_row = pl.multiple_of(8 * step, 8)
            up = rise[pl.ds(first_row, 8), lanes]
            far = fall[pl.ds(first_row, 8), lanes]
            for k in range(8):
                i = first_row + k
                grown = up[k:k + 1] * o
                total = grown + inw[t, i] + far[k:k + 1] * in_carry
                coef[t, pl.ds(i, FUNCS, stride=ROWS), :] = multipole * total
                o = grown + src[t, i]
            return o

        lax.fori_loop(0, ROWS // 8, forth, out_carry)

    for peer in fn_peers:
        pltpu.make_async_remote_copy(
            src_ref=x_buf.at[peer], dst_ref=x_in.at[fn], send_sem=x_send.at[peer], recv_sem=x_recv.at[fn],
            device_id=(rad, peer), device_id_type=MESH,
        ).start()
    x_in[fn] = x_buf[fn]

    @pl.loop(0, FUNCS // 4)
    def _(quad):
        at = pl.ds(pl.multiple_of(quad * 160, 16), 160)
        left = jnp.concatenate([coef[t, at, :].astype(BF16) for t in range(2 * CHUNKS)], axis=1)[:, :HARM]
        out = lax.dot_general(left, ylm_v[...], (((1,), (1,)), ((), ())), preferred_element_type=F32)
        potential[pl.ds(4 * quad, 4)] = out.reshape(4, ROWS, ANGLES).astype(BF16)

    def gram_of(left, right):
        return lax.dot_general(left, right, (((1,), (1,)), ((), ())), preferred_element_type=F32)

    for c in range(CHUNKS):
        for peer in fn_peers:
            y_copy(c, peer, peer).wait_recv()
        x = jnp.concatenate([y_in[c, :, t].reshape(FNS * FUNCS, 128) for t in range(TILES[c])], axis=1)
        if c == 0:
            gram[...] = gram_of(x, x)
        else:
            gram[...] += gram_of(x, x)

    for peer in fn_peers:
        pltpu.make_async_remote_copy(
            src_ref=x_buf.at[peer], dst_ref=x_in.at[peer], send_sem=x_send.at[peer], recv_sem=x_recv.at[peer],
            device_id=(rad, peer), device_id_type=MESH,
        ).wait_recv()
    x = x_in[...].reshape(FNS * FUNCS, 128)
    part[...] = (gram[...] + gram_of(x, jnp.concatenate([x[:, 64:], x[:, :64]], axis=1))).astype(BF16)

    def part_copy(peer, slot):
        return pltpu.make_async_remote_copy(
            src_ref=part.at[pl.ds(pl.multiple_of(peer * FUNCS, 16), FUNCS)], dst_ref=part_in.at[slot],
            send_sem=p_send.at[peer], recv_sem=p_recv.at[slot], device_id=(peer, fn), device_id_type=MESH,
        )

    @pl.loop(1, RADS)
    def _(step):
        part_copy(lax.rem(rad + step, RADS), rad).start()

    part_in[rad] = part[pl.ds(pl.multiple_of(rad * FUNCS, 16), FUNCS), :]

    @pl.loop(1, RADS)
    def _(step):
        peer = lax.rem(rad + step, RADS)
        part_copy(peer, peer).wait_recv()

    total = part_in[0].astype(F32)
    for b in range(1, RADS):
        total = total + part_in[b].astype(F32)
    for h in range(2):
        for q in range(2):
            tile = swap_blocks(total[8 * h:8 * h + 8, 128 * q:128 * q + 128])
            for k in range(8):
                slab[8 * q + k, h:h + 1, :] = tile[k:k + 1, :]

    def slab_copy(peer, slot):
        return pltpu.make_async_remote_copy(
            src_ref=slab.at[peer], dst_ref=slab_in.at[slot], send_sem=s_send.at[peer],
            recv_sem=s_recv.at[slot], device_id=(rad, peer), device_id_type=MESH,
        )

    for peer in fn_peers:
        slab_copy(peer, fn).start()
    slab_in[fn] = slab[fn]
    for peer in fn_peers:
        slab_copy(peer, peer).wait_recv()
    total = slab_in[0]
    for b in range(1, FNS):
        total = total + slab_in[b]
    for h in range(2):
        tile = swap_blocks(jnp.broadcast_to(total[h:h + 1], (8, 128)))
        matrix[8 * h:8 * h + 8, :] = tile[:, :FUNCS]

    for peer in fn_peers:
        for c in range(CHUNKS):
            y_copy(c, peer, fn).wait_send()
        pltpu.make_async_remote_copy(
            src_ref=x_buf.at[peer], dst_ref=x_in.at[fn], send_sem=x_send.at[peer], recv_sem=x_recv.at[fn],
            device_id=(rad, peer), device_id_type=MESH,
        ).wait_send()
        slab_copy(peer, fn).wait_send()

    @pl.loop(1, RADS)
    def _(step):
        peer = lax.rem(rad + step, RADS)
        pltpu.make_async_remote_copy(
            src_ref=edge.at[0], dst_ref=edge_in.at[rad], send_sem=e_send.at[peer], recv_sem=e_recv.at[rad],
            device_id=(peer, fn), device_id_type=MESH,
        ).wait_send()
        part_copy(peer, rad).wait_send()


def local(functions, orbital, radial_weight, ylm):
    hbm = pl.BlockSpec(memory_space=pltpu.HBM)
    vmem, dma = pltpu.VMEM, pltpu.SemaphoreType.DMA
    lanes = CHUNKS * WIDE
    return pl.pallas_call(
        kernel,
        out_shape=(vmem((FUNCS, ROWS, ANGLES), BF16), vmem((FUNCS, FUNCS), F32)),
        in_specs=[hbm, hbm, pl.BlockSpec(memory_space=pltpu.SMEM), hbm],
        out_specs=(pl.BlockSpec(memory_space=pltpu.VMEM), pl.BlockSpec(memory_space=pltpu.VMEM)),
        scratch_shapes=[
            vmem((FUNCS, ROWS, ANGLES), BF16),
            vmem((ROWS, ANGLES), F32),
            vmem((ANGLES, HARM), BF16),
            vmem((FUNCS * ROWS, ANGLES), BF16),
            vmem((2, FUNCS * ROWS, 128), F32),
            vmem((2 * CHUNKS, ROWS, FUNCS, 128), F32),
            vmem((2 * CHUNKS, ROWS, FUNCS, 128), F32),
            vmem((2 * CHUNKS, FUNCS * ROWS, 128), F32),
            vmem((ROWS, lanes), F32),
            vmem((ROWS, lanes), F32),
            vmem((ROWS, lanes), F32),
            vmem((ROWS, lanes), F32),
            vmem((RADS, lanes), F32),
            vmem((RADS, lanes), F32),
            vmem((CHUNKS, 2 * ROWS, FUNCS, 128), BF16),
            vmem((CHUNKS, FNS, max(TILES), FUNCS, 128), BF16),
            vmem((FNS, FUNCS, 128), BF16),
            vmem((FNS, FUNCS, 128), BF16),
            vmem((2, FUNCS, lanes), BF16),
            vmem((RADS, FUNCS, lanes), BF16),
            vmem((FNS * FUNCS, FNS * FUNCS), F32),
            vmem((FNS * FUNCS, FNS * FUNCS), BF16),
            vmem((RADS, FUNCS, FNS * FUNCS), BF16),
            vmem((FNS, 2, 128), F32),
            vmem((FNS, 2, 128), F32),
            dma((3,)),
            dma((CHUNKS, FNS)), dma((CHUNKS, FNS)),
            dma((FNS,)), dma((FNS,)),
            dma((RADS,)), dma((RADS,)),
            dma((RADS,)), dma((RADS,)),
            dma((FNS,)), dma((FNS,)),
        ],
        compiler_params=pltpu.CompilerParams(
            collective_id=0, has_side_effects=True, vmem_limit_bytes=61 * 2**20
        ),
    )(functions, orbital, radial_weight, ylm.T)


def solution(mesh):
    in_specs = (P("fn", "rad", None), P("rad", None), P("rad"), P())
    out_specs = (P("fn", "rad", None), P("rad", "fn"))
    return jax.shard_map(local, mesh=mesh, in_specs=in_specs, out_specs=out_specs, check_vma=False)
```

```python
import functools
import math

import jax
import jax.numpy as jnp
from jax import lax
from jax.experimental import pallas as pl
from jax.experimental.pallas import tpu as pltpu
from jax.sharding import PartitionSpec as P

MESH = pl.DeviceIdType.MESH
F32, BF16 = jnp.float32, jnp.bfloat16
ANGLES, HARM, RADII = 1202, 961, 640
RADS, FNS = 16, 16
ROWS, FUNCS = 40, 16
SPACING = 3.0 / RADII
CHUNKS, WIDE = 4, 256
TILES = (5, 5, 5, 4)
OWN = 3
FN_STEPS = [(y, z) for z in (4, 3, 5, 2, 6, 1, 7, 0) for y in (0, 1) if (y, z) != (0, 0)]


def degree_of(first, width):
    m = first + lax.broadcasted_iota(jnp.int32, (1, width), 1)
    return jnp.floor(jnp.sqrt(m.astype(F32) + 0.5))


RAD_STEPS = (8, 7, 9, 6, 10, 5, 11, 4, 12, 3, 13, 2, 14, 1, 15)


def swap_blocks(x):
    row = lax.broadcasted_iota(jnp.int32, (8, 128), 0)
    block = lax.broadcasted_iota(jnp.int32, (8, 128), 1) // 16
    for b in (1, 2, 4):
        row_bit, block_bit = (row // b) % 2, (block // b) % 2
        above = pltpu.roll(pltpu.roll(x, 8 - b, 0), 16 * b, 1)
        below = pltpu.roll(pltpu.roll(x, b, 0), 128 - 16 * b, 1)
        x = jnp.where(row_bit == block_bit, x, jnp.where(block_bit == 1, above, below))
    return x


def kernel(
    functions, orbital, weight, ylm,
    potential, matrix,
    fn_v, orb_v, ylm_v, dens, proj, src, inw, coef,
    decay, rise, scale, fall, couple_o, couple_n,
    y_buf, y_in, x_buf, x_in, edge, edge_in, gram, part, part_in, slab, slab_in,
    load_sem, y_send, y_recv, x_send, x_recv, e_send, e_recv, p_send, p_recv, s_send, s_recv,
):
    rad, fn = lax.axis_index("rad"), lax.axis_index("fn")
    fn_y, fn_z = fn // 8, lax.rem(fn, 8)
    fn_peers = [lax.rem(fn_y + y, 2) * 8 + lax.rem(fn_z + z, 8) for y, z in FN_STEPS]

    loads = [
        pltpu.make_async_copy(functions, fn_v, load_sem.at[0]),
        pltpu.make_async_copy(orbital, orb_v, load_sem.at[1]),
        pltpu.make_async_copy(ylm, ylm_v, load_sem.at[2]),
    ]
    barrier = pltpu.get_barrier_semaphore()
    for peer in fn_peers:
        pl.semaphore_signal(barrier, inc=1, device_id=(rad, peer), device_id_type=MESH)

    @pl.loop(1, RADS)
    def _(step):
        pl.semaphore_signal(barrier, inc=1, device_id=(lax.rem(rad + step, RADS), fn), device_id_type=MESH)

    for copy in loads:
        copy.start()

    core = lax.rem(rad, 2)

    def share(c, peer):
        y, z = peer // 8, lax.rem(peer, 8)
        return y * 8 + lax.rem(z + 4 * y + 6 * core + 8 - c, 8)

    def first_owner(c, h):
        return h * 8 + lax.rem(4 * h + 2 * core + c, 8)

    def y_copy(c, peer, slot):
        return pltpu.make_async_remote_copy(
            src_ref=y_buf.at[c, pl.ds(share(c, peer) * TILES[c], TILES[c])], dst_ref=y_in.at[c, slot, pl.ds(0, TILES[c])],
            send_sem=y_send.at[c, peer], recv_sem=y_recv.at[c, slot], device_id=(rad, peer), device_id_type=MESH,
        )

    def x_copy(t, peer, slot):
        return pltpu.make_async_remote_copy(
            src_ref=x_buf.at[t], dst_ref=x_in.at[slot], send_sem=x_send.at[t], recv_sem=x_recv.at[slot],
            device_id=(rad, peer), device_id_type=MESH,
        )

    def radius_of(position):
        return 1.0 + SPACING * (position.astype(F32) + 0.5)

    def minus_log(x):
        return x * (1.0 + x * (0.5 + x * (1.0 / 3.0 + x * 0.25)))

    rows = lax.broadcasted_iota(jnp.int32, (ROWS, 1), 0)
    radius = radius_of(rad * ROWS + rows)
    gap = SPACING / radius
    step_log = minus_log(gap)
    next_log = minus_log(SPACING / radius_of(rad * ROWS + rows + 1))
    for c in range(CHUNKS):
        lanes = pl.ds(c * WIDE, WIDE)
        deg = degree_of(c * WIDE, WIDE)
        decay[:, lanes] = jnp.exp(-deg * next_log)
        rise[:, lanes] = jnp.exp(-deg * step_log) * (1.0 - gap)
        t = (2.0 * deg + 1.0) * step_log
        em = t * (1.0 - t * (1 / 2) * (1.0 - t * (1 / 3) * (1.0 - t * (1 / 4) * (1.0 - t * (1 / 5) * (1.0 - t * (1 / 6) * (1.0 - t * (1 / 7)))))))
        em = jnp.where(rows + (0 if c < OWN else rad * ROWS) == 0, 1.0, em)
        scale[:, lanes] = jnp.sqrt((16.0 * math.pi**2 / ANGLES) / (2.0 * deg + 1.0) * radius * em)

    for copy in loads[:2]:
        copy.wait()
    orb = orb_v[...]

    @pl.loop(0, FUNCS // 2)
    def _(pair):
        d = fn_v[pl.ds(2 * pair, 2)].astype(F32) * orb[None]
        dens[pl.ds(pl.multiple_of(pair * 80, 16), 80), :] = d.reshape(80, ANGLES).astype(BF16)

    loads[2].wait()

    lane = lax.broadcasted_iota(jnp.int32, (FUNCS, 128), 1)

    def put_tiles(c, first_row, k, ys, odd, spare):
        i = first_row + k
        if c < CHUNKS - 1:
            for h in range(2):
                y_buf[c, ROWS * h + i] = ys[h].astype(BF16)
            return odd, spare
        y_buf[c, i] = ys[0].astype(BF16)
        spare = jnp.where(lane == i, ys[1][:, 64:65], spare)
        if k % 2:
            y_buf[c, ROWS + first_row // 2 + k // 2] = jnp.where(lane < 64, odd, pltpu.roll(ys[1], 64, 1)).astype(BF16)
        return ys[1], spare

    def send_chunk(c):
        for peer in fn_peers:
            y_copy(c, peer, fn).start()
        y_in[c, fn, 0:TILES[c]] = y_buf[c, pl.ds(share(c, fn) * TILES[c], TILES[c])]

    for c in range(CHUNKS):
        width = min(WIDE, HARM - c * WIDE)
        out = lax.dot_general(
            dens[...], ylm_v[:, c * WIDE:c * WIDE + width], (((1,), (0,)), ((), ())), preferred_element_type=F32
        )
        if width == WIDE:
            proj[0] = out[:, :128]
            proj[1] = out[:, 128:]
        else:
            proj[0] = out[:, :128]
            proj[1] = jnp.zeros_like(proj[1])
            proj[1, :, 0:width - 128] = out[:, 128:]

        base = c * WIDE

        def back(step, n):
            first_row = pl.multiple_of(8 * (ROWS // 8 - 1 - step), 8)
            down = decay[pl.ds(first_row, 8), base:base + WIDE]
            up = scale[pl.ds(first_row, 8), base:base + WIDE]
            for k in reversed(range(8)):
                i = first_row + k
                r_i = 1.0 + SPACING * ((rad * ROWS + i).astype(F32) + 0.5)
                factor = SPACING * weight[i] * r_i
                new = []
                for h in range(2):
                    lanes = slice(128 * h, 128 * h + 128)
                    s = proj[h, pl.ds(i, FUNCS, stride=ROWS), :] * factor
                    src[2 * c + h, i] = s
                    v = s + down[k:k + 1, lanes] * n[h]
                    inw[2 * c + h, i] = v
                    new.append(v)
                if c < OWN:
                    put_tiles(c, first_row, k, [new[h] * up[k:k + 1, 128 * h:128 * h + 128] for h in range(2)], None, None)
                n = tuple(new)
            return n

        zero = jnp.zeros((FUNCS, 128), F32)
        first = lax.fori_loop(0, ROWS // 8, back, (zero, zero))
        for h in range(2):
            edge[1, :, base + 128 * h:base + 128 * h + 128] = first[h].astype(BF16)

        if c == 0:
            pl.semaphore_wait(barrier, len(FN_STEPS) + RADS - 1)
        if c < OWN:
            send_chunk(c)

        def forth(step, o):
            first_row = pl.multiple_of(8 * step, 8)
            up = rise[pl.ds(first_row, 8), base:base + WIDE]
            for k in range(8):
                o = tuple(
                    src[2 * c + h, first_row + k] + up[k:k + 1, 128 * h:128 * h + 128] * o[h] for h in range(2)
                )
            return o

        last = lax.fori_loop(0, ROWS // 8, forth, (zero, zero))
        for h in range(2):
            edge[0, :, base + 128 * h:base + 128 * h + 128] = last[h].astype(BF16)

    @pl.loop(1, RADS)
    def _(step):
        peer = lax.rem(rad + step, RADS)
        pltpu.make_async_remote_copy(
            src_ref=edge.at[jnp.where(peer > rad, 0, 1)],
            dst_ref=edge_in.at[rad],
            send_sem=e_send.at[peer],
            recv_sem=e_recv.at[rad],
            device_id=(peer, fn),
            device_id_type=MESH,
        ).start()

    edge_in[rad] = jnp.zeros((FUNCS, CHUNKS * WIDE), BF16)
    blocks = lax.broadcasted_iota(jnp.int32, (RADS, 1), 0)
    log_last = jnp.log(radius_of(blocks * ROWS + (ROWS - 1)))
    log_first = jnp.log(radius_of(blocks * ROWS))
    spot = jnp.full((1, 1), rad, jnp.int32)
    log_end = jnp.log(radius_of(spot * ROWS - 1))
    log_next = jnp.log(radius_of(spot * ROWS + ROWS))
    log_row = jnp.log(radius)
    for c in range(CHUNKS):
        lanes = pl.ds(c * WIDE, WIDE)
        deg = degree_of(c * WIDE, WIDE)
        couple_o[:, lanes] = jnp.where(blocks < spot, jnp.exp((deg + 1.0) * jnp.minimum(log_last - log_end, 0.0)), 0.0)
        couple_n[:, lanes] = jnp.where(blocks > spot, jnp.exp(deg * jnp.minimum(log_next - log_first, 0.0)), 0.0)
        fall[:, lanes] = jnp.exp(deg * jnp.minimum(log_row - log_next, 0.0))

    @pl.loop(1, RADS)
    def _(step):
        peer = lax.rem(rad + step, RADS)
        pltpu.make_async_remote_copy(
            src_ref=edge.at[0], dst_ref=edge_in.at[peer], send_sem=e_send.at[peer], recv_sem=e_recv.at[peer],
            device_id=(peer, fn), device_id_type=MESH,
        ).wait_recv()

    carries = []
    for t in range(2 * CHUNKS):
        lanes = slice(128 * t, 128 * t + 128)
        out_carry = jnp.zeros((FUNCS, 128), F32)
        in_carry = jnp.zeros((FUNCS, 128), F32)
        for b in range(RADS):
            e = edge_in[b, :, lanes].astype(F32)
            out_carry = out_carry + couple_o[b:b + 1, lanes] * e
            in_carry = in_carry + couple_n[b:b + 1, lanes] * e
        carries.append((out_carry, in_carry))
        if t < 2 * OWN:
            x_buf[t] = (out_carry * (scale[0:1, lanes] * rise[0:1, lanes])).astype(BF16)

    for c in range(OWN, CHUNKS):
        base = c * WIDE

        def whole(step, spare):
            first_row = pl.multiple_of(8 * step, 8)
            up = scale[pl.ds(first_row, 8), base:base + WIDE]
            far = fall[pl.ds(first_row, 8), base:base + WIDE]
            odd = None
            for k in range(8):
                ys = []
                for h in range(2):
                    lanes = slice(128 * h, 128 * h + 128)
                    v = inw[2 * c + h, first_row + k] + far[k:k + 1, lanes] * carries[2 * c + h][1]
                    ys.append(v * up[k:k + 1, lanes])
                odd, spare = put_tiles(c, first_row, k, ys, odd, spare)
            return spare

        spare = lax.fori_loop(0, ROWS // 8, whole, jnp.zeros((FUNCS, 128), F32))
        if c == CHUNKS - 1:
            y_buf[c, ROWS + ROWS // 2] = spare.astype(BF16)
            y_buf[c, ROWS + ROWS // 2 + 1:FNS * TILES[c]] = jnp.zeros((3, FUNCS, 128), BF16)
        send_chunk(c)
        if c == OWN:
            for t in range(2 * OWN):
                owner = first_owner(t // 2, t % 2)

                @pl.when(owner != fn)
                def _():
                    x_copy(t, owner, fn).start()

                @pl.when(owner == fn)
                def _():
                    x_in[fn] = x_buf[t]

    for t in range(2 * CHUNKS):
        lanes = slice(128 * t, 128 * t + 128)
        multipole = (4.0 * math.pi) / (2.0 * degree_of(128 * t, 128) + 1.0)
        out_carry, in_carry = carries[t]

        def forth(step, o):
            first_row = pl.multiple_of(8 * step, 8)
            up = rise[pl.ds(first_row, 8), lanes]
            far = fall[pl.ds(first_row, 8), lanes]
            for k in range(8):
                i = first_row + k
                grown = up[k:k + 1] * o
                total = grown + inw[t, i] + far[k:k + 1] * in_carry
                coef[t, pl.ds(i, FUNCS, stride=ROWS), :] = multipole * total
                o = grown + src[t, i]
            return o

        lax.fori_loop(0, ROWS // 8, forth, out_carry)

    @pl.loop(0, FUNCS // 4)
    def _(quad):
        at = pl.ds(pl.multiple_of(quad * 160, 16), 160)
        left = jnp.concatenate([coef[t, at, :].astype(BF16) for t in range(2 * CHUNKS)], axis=1)[:, :HARM]
        out = lax.dot_general(left, ylm_v[...], (((1,), (1,)), ((), ())), preferred_element_type=F32)
        potential[pl.ds(4 * quad, 4)] = out.reshape(4, ROWS, ANGLES).astype(BF16)

    def gram_of(left, right):
        return lax.dot_general(left, right, (((1,), (1,)), ((), ())), preferred_element_type=F32)

    for c in range(CHUNKS):
        for peer in fn_peers:
            y_copy(c, peer, peer).wait_recv()
        x = jnp.concatenate([y_in[c, :, t].reshape(FNS * FUNCS, 128) for t in range(TILES[c])], axis=1)
        if c == 0:
            gram[...] = gram_of(x, x)
        elif c < CHUNKS - 1:
            gram[...] += gram_of(x, x)
        else:
            part[...] = (gram[...] + gram_of(x, x)).astype(BF16)
        if c == CHUNKS - 2:
            for t in range(2 * OWN):

                @pl.when(first_owner(t // 2, t % 2) == fn)
                def _():
                    for peer in fn_peers:
                        x_copy(t, peer, peer).wait_recv()
                    p = x_in[...].reshape(FNS * FUNCS, 128)
                    a = y_in[t // 2, :, 0].reshape(FNS * FUNCS, 128)
                    gram[...] += gram_of(a, p) + gram_of(p, a)

    def part_copy(peer, slot):
        return pltpu.make_async_remote_copy(
            src_ref=part.at[pl.ds(pl.multiple_of(peer * FUNCS, 16), FUNCS)], dst_ref=part_in.at[slot],
            send_sem=p_send.at[peer], recv_sem=p_recv.at[slot], device_id=(peer, fn), device_id_type=MESH,
        )

    rad_peers = [lax.rem(rad + step, RADS) for step in RAD_STEPS]
    for peer in rad_peers:
        part_copy(peer, rad).start()

    part_in[rad] = part[pl.ds(pl.multiple_of(rad * FUNCS, 16), FUNCS), :]

    for peer in rad_peers:
        part_copy(peer, peer).wait_recv()

    total = part_in[0].astype(F32)
    for b in range(1, RADS):
        total = total + part_in[b].astype(F32)
    for h in range(2):
        for q in range(2):
            tile = swap_blocks(total[8 * h:8 * h + 8, 128 * q:128 * q + 128])
            for k in range(8):
                slab[8 * q + k, h:h + 1, :] = tile[k:k + 1, :]

    def slab_copy(peer, slot):
        return pltpu.make_async_remote_copy(
            src_ref=slab.at[peer], dst_ref=slab_in.at[slot], send_sem=s_send.at[peer],
            recv_sem=s_recv.at[slot], device_id=(rad, peer), device_id_type=MESH,
        )

    for peer in fn_peers:
        slab_copy(peer, fn).start()
    slab_in[fn] = slab[fn]
    for peer in fn_peers:
        slab_copy(peer, peer).wait_recv()
    total = slab_in[0]
    for b in range(1, FNS):
        total = total + slab_in[b]
    for h in range(2):
        tile = swap_blocks(jnp.broadcast_to(total[h:h + 1], (8, 128)))
        matrix[8 * h:8 * h + 8, :] = tile[:, :FUNCS]

    for peer in fn_peers:
        for c in range(CHUNKS):
            y_copy(c, peer, fn).wait_send()
        slab_copy(peer, fn).wait_send()
    for t in range(2 * OWN):
        owner = first_owner(t // 2, t % 2)

        @pl.when(owner != fn)
        def _():
            x_copy(t, owner, fn).wait_send()

    @pl.loop(1, RADS)
    def _(step):
        peer = lax.rem(rad + step, RADS)
        pltpu.make_async_remote_copy(
            src_ref=edge.at[0], dst_ref=edge_in.at[rad], send_sem=e_send.at[peer], recv_sem=e_recv.at[rad],
            device_id=(peer, fn), device_id_type=MESH,
        ).wait_send()
        part_copy(peer, rad).wait_send()


def local(functions, orbital, radial_weight, ylm):
    hbm = pl.BlockSpec(memory_space=pltpu.HBM)
    vmem, dma = pltpu.VMEM, pltpu.SemaphoreType.DMA
    lanes = CHUNKS * WIDE
    return pl.pallas_call(
        kernel,
        out_shape=(vmem((FUNCS, ROWS, ANGLES), BF16), vmem((FUNCS, FUNCS), F32)),
        in_specs=[hbm, hbm, pl.BlockSpec(memory_space=pltpu.SMEM), hbm],
        out_specs=(pl.BlockSpec(memory_space=pltpu.VMEM), pl.BlockSpec(memory_space=pltpu.VMEM)),
        scratch_shapes=[
            vmem((FUNCS, ROWS, ANGLES), BF16),
            vmem((ROWS, ANGLES), F32),
            vmem((ANGLES, HARM), BF16),
            vmem((FUNCS * ROWS, ANGLES), BF16),
            vmem((2, FUNCS * ROWS, 128), F32),
            vmem((2 * CHUNKS, ROWS, FUNCS, 128), F32),
            vmem((2 * CHUNKS, ROWS, FUNCS, 128), F32),
            vmem((2 * CHUNKS, FUNCS * ROWS, 128), F32),
            vmem((ROWS, lanes), F32),
            vmem((ROWS, lanes), F32),
            vmem((ROWS, lanes), F32),
            vmem((ROWS, lanes), F32),
            vmem((RADS, lanes), F32),
            vmem((RADS, lanes), F32),
            vmem((CHUNKS, 2 * ROWS, FUNCS, 128), BF16),
            vmem((CHUNKS, FNS, max(TILES), FUNCS, 128), BF16),
            vmem((2 * OWN, FUNCS, 128), BF16),
            vmem((FNS, FUNCS, 128), BF16),
            vmem((2, FUNCS, lanes), BF16),
            vmem((RADS, FUNCS, lanes), BF16),
            vmem((FNS * FUNCS, FNS * FUNCS), F32),
            vmem((FNS * FUNCS, FNS * FUNCS), BF16),
            vmem((RADS, FUNCS, FNS * FUNCS), BF16),
            vmem((FNS, 2, 128), F32),
            vmem((FNS, 2, 128), F32),
            dma((3,)),
            dma((CHUNKS, FNS)), dma((CHUNKS, FNS)),
            dma((2 * OWN,)), dma((FNS,)),
            dma((RADS,)), dma((RADS,)),
            dma((RADS,)), dma((RADS,)),
            dma((FNS,)), dma((FNS,)),
        ],
        compiler_params=pltpu.CompilerParams(
            collective_id=0, has_side_effects=True, vmem_limit_bytes=61 * 2**20
        ),
    )(functions, orbital, radial_weight, ylm.T)


def solution(mesh):
    in_specs = (P("fn", "rad", None), P("rad", None), P("rad"), P())
    out_specs = (P("fn", "rad", None), P("rad", "fn"))
    return jax.shard_map(local, mesh=mesh, in_specs=in_specs, out_specs=out_specs, check_vma=False)
```

```python
import functools
import math

import jax
import jax.numpy as jnp
from jax import lax
from jax.experimental import pallas as pl
from jax.experimental.pallas import tpu as pltpu
from jax.sharding import PartitionSpec as P

MESH = pl.DeviceIdType.MESH
F32, BF16 = jnp.float32, jnp.bfloat16
ANGLES, HARM, RADII = 1202, 961, 640
RADS, FNS = 16, 16
ROWS, FUNCS = 40, 16
SPACING = 3.0 / RADII
CHUNKS, WIDE = 4, 256
TILES = (5, 5, 5, 4)
OWN = 3
FN_STEPS = [(y, z) for z in (4, 3, 5, 2, 6, 1, 7, 0) for y in (0, 1) if (y, z) != (0, 0)]


def degree_of(first, width):
    m = first + lax.broadcasted_iota(jnp.int32, (1, width), 1)
    return jnp.floor(jnp.sqrt(m.astype(F32) + 0.5))


RAD_STEPS = (8, 7, 9, 6, 10, 5, 11, 4, 12, 3, 13, 2, 14, 1, 15)


def swap_blocks(x):
    row = lax.broadcasted_iota(jnp.int32, (8, 128), 0)
    block = lax.broadcasted_iota(jnp.int32, (8, 128), 1) // 16
    for b in (1, 2, 4):
        row_bit, block_bit = (row // b) % 2, (block // b) % 2
        above = pltpu.roll(pltpu.roll(x, 8 - b, 0), 16 * b, 1)
        below = pltpu.roll(pltpu.roll(x, b, 0), 128 - 16 * b, 1)
        x = jnp.where(row_bit == block_bit, x, jnp.where(block_bit == 1, above, below))
    return x


def kernel(
    functions, orbital, weight, ylm,
    potential, matrix,
    fn_v, orb_v, ylm_v, dens, proj, src, inw, coef,
    decay, rise, scale, fall, couple_o, couple_n,
    y_buf, y_in, x_buf, x_in, edge, edge_in, gram, part, part_in, slab, slab_in,
    load_sem, y_send, y_recv, x_send, x_recv, e_send, e_recv, p_send, p_recv, s_send, s_recv,
):
    rad, fn = lax.axis_index("rad"), lax.axis_index("fn")
    fn_y, fn_z = fn // 8, lax.rem(fn, 8)
    fn_peers = [lax.rem(fn_y + y, 2) * 8 + lax.rem(fn_z + z, 8) for y, z in FN_STEPS]

    loads = [
        pltpu.make_async_copy(functions, fn_v, load_sem.at[0]),
        pltpu.make_async_copy(orbital, orb_v, load_sem.at[1]),
        pltpu.make_async_copy(ylm, ylm_v, load_sem.at[2]),
    ]
    barrier = pltpu.get_barrier_semaphore()
    for peer in fn_peers:
        pl.semaphore_signal(barrier, inc=1, device_id=(rad, peer), device_id_type=MESH)

    @pl.loop(1, RADS)
    def _(step):
        pl.semaphore_signal(barrier, inc=1, device_id=(lax.rem(rad + step, RADS), fn), device_id_type=MESH)

    for copy in loads:
        copy.start()

    core = lax.rem(rad, 2)

    def share(c, peer):
        y, z = peer // 8, lax.rem(peer, 8)
        return y * 8 + lax.rem(z + 4 * y + 6 * core + 8 - c, 8)

    def first_owner(c, h):
        return h * 8 + lax.rem(4 * h + 2 * core + c, 8)

    def y_copy(c, peer, slot):
        return pltpu.make_async_remote_copy(
            src_ref=y_buf.at[c, pl.ds(share(c, peer) * TILES[c], TILES[c])], dst_ref=y_in.at[c, slot, pl.ds(0, TILES[c])],
            send_sem=y_send.at[c, peer], recv_sem=y_recv.at[c, slot], device_id=(rad, peer), device_id_type=MESH,
        )

    def x_copy(t, peer, slot):
        return pltpu.make_async_remote_copy(
            src_ref=x_buf.at[t], dst_ref=x_in.at[slot], send_sem=x_send.at[t], recv_sem=x_recv.at[slot],
            device_id=(rad, peer), device_id_type=MESH,
        )

    def radius_of(position):
        return 1.0 + SPACING * (position.astype(F32) + 0.5)

    def minus_log(x):
        return x * (1.0 + x * (0.5 + x * (1.0 / 3.0 + x * 0.25)))

    rows = lax.broadcasted_iota(jnp.int32, (ROWS, 1), 0)
    radius = radius_of(rad * ROWS + rows)
    gap = SPACING / radius
    step_log = minus_log(gap)
    next_log = minus_log(SPACING / radius_of(rad * ROWS + rows + 1))
    for c in range(CHUNKS):
        lanes = pl.ds(c * WIDE, WIDE)
        deg = degree_of(c * WIDE, WIDE)
        decay[:, lanes] = jnp.exp(-deg * next_log)
        rise[:, lanes] = jnp.exp(-deg * step_log) * (1.0 - gap)
        t = (2.0 * deg + 1.0) * step_log
        em = t * (1.0 - t * (1 / 2) * (1.0 - t * (1 / 3) * (1.0 - t * (1 / 4) * (1.0 - t * (1 / 5) * (1.0 - t * (1 / 6) * (1.0 - t * (1 / 7)))))))
        em = jnp.where(rows + (0 if c < OWN else rad * ROWS) == 0, 1.0, em)
        scale[:, lanes] = jnp.sqrt((16.0 * math.pi**2 / ANGLES) / (2.0 * deg + 1.0) * radius * em)

    for copy in loads[:2]:
        copy.wait()
    orb = orb_v[...]

    @pl.loop(0, FUNCS // 2)
    def _(pair):
        d = fn_v[pl.ds(2 * pair, 2)].astype(F32) * orb[None]
        dens[pl.ds(pl.multiple_of(pair * 80, 16), 80), :] = d.reshape(80, ANGLES).astype(BF16)

    loads[2].wait()

    lane = lax.broadcasted_iota(jnp.int32, (FUNCS, 128), 1)

    def put_tiles(c, first_row, k, ys, odd, spare):
        i = first_row + k
        if c < CHUNKS - 1:
            for h in range(2):
                y_buf[c, ROWS * h + i] = ys[h].astype(BF16)
            return odd, spare
        y_buf[c, i] = ys[0].astype(BF16)
        spare = jnp.where(lane == i, ys[1][:, 64:65], spare)
        if k % 2:
            y_buf[c, ROWS + first_row // 2 + k // 2] = jnp.where(lane < 64, odd, pltpu.roll(ys[1], 64, 1)).astype(BF16)
        return ys[1], spare

    def send_chunk(c):
        for peer in fn_peers:
            y_copy(c, peer, fn).start()
        y_in[c, fn, 0:TILES[c]] = y_buf[c, pl.ds(share(c, fn) * TILES[c], TILES[c])]

    for c in range(CHUNKS):
        width = min(WIDE, HARM - c * WIDE)
        out = lax.dot_general(
            dens[...], ylm_v[:, c * WIDE:c * WIDE + width], (((1,), (0,)), ((), ())), preferred_element_type=F32
        )
        if width == WIDE:
            proj[0] = out[:, :128]
            proj[1] = out[:, 128:]
        else:
            proj[0] = out[:, :128]
            proj[1] = jnp.zeros_like(proj[1])
            proj[1, :, 0:width - 128] = out[:, 128:]

        base = c * WIDE

        def back(step, n):
            first_row = pl.multiple_of(8 * (ROWS // 8 - 1 - step), 8)
            down = decay[pl.ds(first_row, 8), base:base + WIDE]
            up = scale[pl.ds(first_row, 8), base:base + WIDE]
            for k in reversed(range(8)):
                i = first_row + k
                r_i = 1.0 + SPACING * ((rad * ROWS + i).astype(F32) + 0.5)
                factor = SPACING * weight[i] * r_i
                new = []
                for h in range(2):
                    lanes = slice(128 * h, 128 * h + 128)
                    s = proj[h, pl.ds(i, FUNCS, stride=ROWS), :] * factor
                    src[2 * c + h, i] = s
                    v = s + down[k:k + 1, lanes] * n[h]
                    inw[2 * c + h, i] = v
                    new.append(v)
                if c < OWN:
                    put_tiles(c, first_row, k, [new[h] * up[k:k + 1, 128 * h:128 * h + 128] for h in range(2)], None, None)
                n = tuple(new)
            return n

        zero = jnp.zeros((FUNCS, 128), F32)
        first = lax.fori_loop(0, ROWS // 8, back, (zero, zero))
        for h in range(2):
            edge[1, :, base + 128 * h:base + 128 * h + 128] = first[h].astype(BF16)

        if c == 0:
            pl.semaphore_wait(barrier, len(FN_STEPS) + RADS - 1)
        if c < OWN:
            send_chunk(c)

        def forth(step, o):
            first_row = pl.multiple_of(8 * step, 8)
            up = rise[pl.ds(first_row, 8), base:base + WIDE]
            for k in range(8):
                o = tuple(
                    src[2 * c + h, first_row + k] + up[k:k + 1, 128 * h:128 * h + 128] * o[h] for h in range(2)
                )
            return o

        last = lax.fori_loop(0, ROWS // 8, forth, (zero, zero))
        for h in range(2):
            edge[0, :, base + 128 * h:base + 128 * h + 128] = last[h].astype(BF16)

    @pl.loop(1, RADS)
    def _(step):
        peer = lax.rem(rad + step, RADS)
        pltpu.make_async_remote_copy(
            src_ref=edge.at[jnp.where(peer > rad, 0, 1)],
            dst_ref=edge_in.at[rad],
            send_sem=e_send.at[peer],
            recv_sem=e_recv.at[rad],
            device_id=(peer, fn),
            device_id_type=MESH,
        ).start()

    edge_in[rad] = jnp.zeros((FUNCS, CHUNKS * WIDE), BF16)
    blocks = lax.broadcasted_iota(jnp.int32, (RADS, 1), 0)
    log_last = jnp.log(radius_of(blocks * ROWS + (ROWS - 1)))
    log_first = jnp.log(radius_of(blocks * ROWS))
    spot = jnp.full((1, 1), rad, jnp.int32)
    log_end = jnp.log(radius_of(spot * ROWS - 1))
    log_next = jnp.log(radius_of(spot * ROWS + ROWS))
    log_row = jnp.log(radius)
    for c in range(CHUNKS):
        lanes = pl.ds(c * WIDE, WIDE)
        deg = degree_of(c * WIDE, WIDE)
        couple_o[:, lanes] = jnp.where(blocks < spot, jnp.exp((deg + 1.0) * jnp.minimum(log_last - log_end, 0.0)), 0.0)
        couple_n[:, lanes] = jnp.where(blocks > spot, jnp.exp(deg * jnp.minimum(log_next - log_first, 0.0)), 0.0)
        fall[:, lanes] = jnp.exp(deg * jnp.minimum(log_row - log_next, 0.0))

    @pl.loop(1, RADS)
    def _(step):
        peer = lax.rem(rad + step, RADS)
        pltpu.make_async_remote_copy(
            src_ref=edge.at[0], dst_ref=edge_in.at[peer], send_sem=e_send.at[peer], recv_sem=e_recv.at[peer],
            device_id=(peer, fn), device_id_type=MESH,
        ).wait_recv()

    carries = []
    for t in range(2 * CHUNKS):
        lanes = slice(128 * t, 128 * t + 128)
        out_carry = jnp.zeros((FUNCS, 128), F32)
        in_carry = jnp.zeros((FUNCS, 128), F32)
        for b in range(RADS):
            e = edge_in[b, :, lanes].astype(F32)
            out_carry = out_carry + couple_o[b:b + 1, lanes] * e
            in_carry = in_carry + couple_n[b:b + 1, lanes] * e
        carries.append((out_carry, in_carry))
        if t < 2 * OWN:
            x_buf[t] = (out_carry * (scale[0:1, lanes] * rise[0:1, lanes])).astype(BF16)

    for c in range(OWN, CHUNKS):
        base = c * WIDE

        def whole(step, spare):
            first_row = pl.multiple_of(8 * step, 8)
            up = scale[pl.ds(first_row, 8), base:base + WIDE]
            far = fall[pl.ds(first_row, 8), base:base + WIDE]
            odd = None
            for k in range(8):
                ys = []
                for h in range(2):
                    lanes = slice(128 * h, 128 * h + 128)
                    v = inw[2 * c + h, first_row + k] + far[k:k + 1, lanes] * carries[2 * c + h][1]
                    ys.append(v * up[k:k + 1, lanes])
                odd, spare = put_tiles(c, first_row, k, ys, odd, spare)
            return spare

        spare = lax.fori_loop(0, ROWS // 8, whole, jnp.zeros((FUNCS, 128), F32))
        if c == CHUNKS - 1:
            y_buf[c, ROWS + ROWS // 2] = spare.astype(BF16)
            y_buf[c, ROWS + ROWS // 2 + 1:FNS * TILES[c]] = jnp.zeros((3, FUNCS, 128), BF16)
        send_chunk(c)
        if c == OWN:
            for t in range(2 * OWN):
                owner = first_owner(t // 2, t % 2)

                @pl.when(owner != fn)
                def _():
                    x_copy(t, owner, fn).start()

                @pl.when(owner == fn)
                def _():
                    x_in[fn] = x_buf[t]

    for t in range(2 * CHUNKS):
        lanes = slice(128 * t, 128 * t + 128)
        multipole = (4.0 * math.pi) / (2.0 * degree_of(128 * t, 128) + 1.0)
        out_carry, in_carry = carries[t]

        def forth(step, o):
            first_row = pl.multiple_of(8 * step, 8)
            up = rise[pl.ds(first_row, 8), lanes]
            far = fall[pl.ds(first_row, 8), lanes]
            for k in range(8):
                i = first_row + k
                grown = up[k:k + 1] * o
                total = grown + inw[t, i] + far[k:k + 1] * in_carry
                coef[t, pl.ds(i, FUNCS, stride=ROWS), :] = multipole * total
                o = grown + src[t, i]
            return o

        lax.fori_loop(0, ROWS // 8, forth, out_carry)

    @pl.loop(0, FUNCS // 4)
    def _(quad):
        at = pl.ds(pl.multiple_of(quad * 160, 16), 160)
        left = jnp.concatenate([coef[t, at, :].astype(BF16) for t in range(2 * CHUNKS)], axis=1)[:, :HARM]
        out = lax.dot_general(left, ylm_v[...], (((1,), (1,)), ((), ())), preferred_element_type=F32)
        potential[pl.ds(4 * quad, 4)] = out.reshape(4, ROWS, ANGLES).astype(BF16)

    @pl.loop(1, RADS)
    def _(step):
        peer = lax.rem(rad + step, RADS)
        pltpu.make_async_remote_copy(
            src_ref=edge.at[0], dst_ref=edge_in.at[rad], send_sem=e_send.at[peer], recv_sem=e_recv.at[rad],
            device_id=(peer, fn), device_id_type=MESH,
        ).wait_send()

    def gram_of(left, right):
        return lax.dot_general(left, right, (((1,), (1,)), ((), ())), preferred_element_type=F32)

    for c in range(CHUNKS):
        for peer in fn_peers:
            y_copy(c, peer, peer).wait_recv()
        x = jnp.concatenate([y_in[c, :, t].reshape(FNS * FUNCS, 128) for t in range(TILES[c])], axis=1)
        if c == 0:
            gram[...] = gram_of(x, x)
        elif c < CHUNKS - 1:
            gram[...] += gram_of(x, x)
        else:
            part[...] = (gram[...] + gram_of(x, x)).astype(BF16)
        if c == CHUNKS - 2:
            for t in range(2 * OWN):

                @pl.when(first_owner(t // 2, t % 2) == fn)
                def _():
                    for peer in fn_peers:
                        x_copy(t, peer, peer).wait_recv()
                    p = x_in[...].reshape(FNS * FUNCS, 128)
                    a = y_in[t // 2, :, 0].reshape(FNS * FUNCS, 128)
                    gram[...] += gram_of(a, p) + gram_of(p, a)

    def part_copy(peer, slot):
        return pltpu.make_async_remote_copy(
            src_ref=part.at[pl.ds(pl.multiple_of(peer * FUNCS, 16), FUNCS)], dst_ref=part_in.at[slot],
            send_sem=p_send.at[peer], recv_sem=p_recv.at[slot], device_id=(peer, fn), device_id_type=MESH,
        )

    rad_peers = [lax.rem(rad + step, RADS) for step in RAD_STEPS]
    for peer in rad_peers:
        part_copy(peer, rad).start()

    for c in range(CHUNKS):
        for peer in fn_peers:
            y_copy(c, peer, fn).wait_send()
    for t in range(2 * OWN):
        owner = first_owner(t // 2, t % 2)

        @pl.when(owner != fn)
        def _():
            x_copy(t, owner, fn).wait_send()


    part_in[rad] = part[pl.ds(pl.multiple_of(rad * FUNCS, 16), FUNCS), :]

    for peer in rad_peers:
        part_copy(peer, peer).wait_recv()

    total = part_in[0].astype(F32)
    for b in range(1, RADS):
        total = total + part_in[b].astype(F32)
    for h in range(2):
        for q in range(2):
            tile = swap_blocks(total[8 * h:8 * h + 8, 128 * q:128 * q + 128])
            for k in range(8):
                slab[8 * q + k, h:h + 1, :] = tile[k:k + 1, :]

    def slab_copy(peer, slot):
        return pltpu.make_async_remote_copy(
            src_ref=slab.at[peer], dst_ref=slab_in.at[slot], send_sem=s_send.at[peer],
            recv_sem=s_recv.at[slot], device_id=(rad, peer), device_id_type=MESH,
        )

    for peer in fn_peers:
        slab_copy(peer, fn).start()
    for peer in rad_peers:
        part_copy(peer, rad).wait_send()
    slab_in[fn] = slab[fn]
    for peer in fn_peers:
        slab_copy(peer, peer).wait_recv()
    total = slab_in[0]
    for b in range(1, FNS):
        total = total + slab_in[b]
    for h in range(2):
        tile = swap_blocks(jnp.broadcast_to(total[h:h + 1], (8, 128)))
        matrix[8 * h:8 * h + 8, :] = tile[:, :FUNCS]

    for peer in fn_peers:
        slab_copy(peer, fn).wait_send()


def local(functions, orbital, radial_weight, ylm):
    hbm = pl.BlockSpec(memory_space=pltpu.HBM)
    vmem, dma = pltpu.VMEM, pltpu.SemaphoreType.DMA
    lanes = CHUNKS * WIDE
    return pl.pallas_call(
        kernel,
        out_shape=(vmem((FUNCS, ROWS, ANGLES), BF16), vmem((FUNCS, FUNCS), F32)),
        in_specs=[hbm, hbm, pl.BlockSpec(memory_space=pltpu.SMEM), hbm],
        out_specs=(pl.BlockSpec(memory_space=pltpu.VMEM), pl.BlockSpec(memory_space=pltpu.VMEM)),
        scratch_shapes=[
            vmem((FUNCS, ROWS, ANGLES), BF16),
            vmem((ROWS, ANGLES), F32),
            vmem((ANGLES, HARM), BF16),
            vmem((FUNCS * ROWS, ANGLES), BF16),
            vmem((2, FUNCS * ROWS, 128), F32),
            vmem((2 * CHUNKS, ROWS, FUNCS, 128), F32),
            vmem((2 * CHUNKS, ROWS, FUNCS, 128), F32),
            vmem((2 * CHUNKS, FUNCS * ROWS, 128), F32),
            vmem((ROWS, lanes), F32),
            vmem((ROWS, lanes), F32),
            vmem((ROWS, lanes), F32),
            vmem((ROWS, lanes), F32),
            vmem((RADS, lanes), F32),
            vmem((RADS, lanes), F32),
            vmem((CHUNKS, 2 * ROWS, FUNCS, 128), BF16),
            vmem((CHUNKS, FNS, max(TILES), FUNCS, 128), BF16),
            vmem((2 * OWN, FUNCS, 128), BF16),
            vmem((FNS, FUNCS, 128), BF16),
            vmem((2, FUNCS, lanes), BF16),
            vmem((RADS, FUNCS, lanes), BF16),
            vmem((FNS * FUNCS, FNS * FUNCS), F32),
            vmem((FNS * FUNCS, FNS * FUNCS), BF16),
            vmem((RADS, FUNCS, FNS * FUNCS), BF16),
            vmem((FNS, 2, 128), F32),
            vmem((FNS, 2, 128), F32),
            dma((3,)),
            dma((CHUNKS, FNS)), dma((CHUNKS, FNS)),
            dma((2 * OWN,)), dma((FNS,)),
            dma((RADS,)), dma((RADS,)),
            dma((RADS,)), dma((RADS,)),
            dma((FNS,)), dma((FNS,)),
        ],
        compiler_params=pltpu.CompilerParams(
            collective_id=0, has_side_effects=True, vmem_limit_bytes=61 * 2**20
        ),
    )(functions, orbital, radial_weight, ylm.T)


def solution(mesh):
    in_specs = (P("fn", "rad", None), P("rad", None), P("rad"), P())
    out_specs = (P("fn", "rad", None), P("rad", "fn"))
    return jax.shard_map(local, mesh=mesh, in_specs=in_specs, out_specs=out_specs, check_vma=False)
```

```python
import functools
import math

import jax
import jax.numpy as jnp
from jax import lax
from jax.experimental import pallas as pl
from jax.experimental.pallas import tpu as pltpu
from jax.sharding import PartitionSpec as P

MESH = pl.DeviceIdType.MESH
F32, BF16 = jnp.float32, jnp.bfloat16
ANGLES, HARM, RADII = 1202, 961, 640
RADS, FNS = 16, 16
ROWS, FUNCS = 40, 16
SPACING = 3.0 / RADII
CHUNKS, WIDE = 4, 256
TILES = (5, 5, 5, 4)
OWN = 3
FN_STEPS = [(y, z) for z in (4, 3, 5, 2, 6, 1, 7, 0) for y in (0, 1) if (y, z) != (0, 0)]


def degree_of(first, width):
    m = first + lax.broadcasted_iota(jnp.int32, (1, width), 1)
    return jnp.floor(jnp.sqrt(m.astype(F32) + 0.5))


RAD_STEPS = (8, 7, 9, 6, 10, 5, 11, 4, 12, 3, 13, 2, 14, 1, 15)


def swap_blocks(x):
    row = lax.broadcasted_iota(jnp.int32, (8, 128), 0)
    block = lax.broadcasted_iota(jnp.int32, (8, 128), 1) // 16
    for b in (1, 2, 4):
        row_bit, block_bit = (row // b) % 2, (block // b) % 2
        above = pltpu.roll(pltpu.roll(x, 8 - b, 0), 16 * b, 1)
        below = pltpu.roll(pltpu.roll(x, b, 0), 128 - 16 * b, 1)
        x = jnp.where(row_bit == block_bit, x, jnp.where(block_bit == 1, above, below))
    return x


def kernel(
    functions, orbital, weight, ylm,
    potential, matrix,
    fn_v, orb_v, ylm_v, dens, proj, src, inw, coef,
    decay, rise, scale, fall, couple_o, couple_n,
    y_buf, y_in, x_buf, x_in, edge, edge_in, gram, part, part_in, slab, slab_in,
    load_sem, y_send, y_recv, x_send, x_recv, e_send, e_recv, p_send, p_recv, s_send, s_recv,
):
    rad, fn = lax.axis_index("rad"), lax.axis_index("fn")
    fn_y, fn_z = fn // 8, lax.rem(fn, 8)
    fn_peers = [lax.rem(fn_y + y, 2) * 8 + lax.rem(fn_z + z, 8) for y, z in FN_STEPS]

    loads = [
        pltpu.make_async_copy(functions, fn_v, load_sem.at[0]),
        pltpu.make_async_copy(orbital, orb_v, load_sem.at[1]),
        pltpu.make_async_copy(ylm, ylm_v, load_sem.at[2]),
    ]
    barrier = pltpu.get_barrier_semaphore()
    for peer in fn_peers:
        pl.semaphore_signal(barrier, inc=1, device_id=(rad, peer), device_id_type=MESH)

    @pl.loop(1, RADS)
    def _(step):
        pl.semaphore_signal(barrier, inc=1, device_id=(lax.rem(rad + step, RADS), fn), device_id_type=MESH)

    for copy in loads:
        copy.start()

    core = lax.rem(rad, 2)

    def share(c, peer):
        y, z = peer // 8, lax.rem(peer, 8)
        return y * 8 + lax.rem(z + 4 * y + 6 * core + 8 - c, 8)

    def first_owner(c, h):
        return h * 8 + lax.rem(4 * h + 2 * core + c, 8)

    def y_copy(c, peer, slot):
        return pltpu.make_async_remote_copy(
            src_ref=y_buf.at[c, pl.ds(share(c, peer) * TILES[c], TILES[c])], dst_ref=y_in.at[c, slot, pl.ds(0, TILES[c])],
            send_sem=y_send.at[c, peer], recv_sem=y_recv.at[c, slot], device_id=(rad, peer), device_id_type=MESH,
        )

    def x_copy(t, peer, slot):
        return pltpu.make_async_remote_copy(
            src_ref=x_buf.at[t], dst_ref=x_in.at[slot], send_sem=x_send.at[t], recv_sem=x_recv.at[slot],
            device_id=(rad, peer), device_id_type=MESH,
        )

    def radius_of(position):
        return 1.0 + SPACING * (position.astype(F32) + 0.5)

    def minus_log(x):
        return x * (1.0 + x * (0.5 + x * (1.0 / 3.0 + x * 0.25)))

    rows = lax.broadcasted_iota(jnp.int32, (ROWS, 1), 0)
    radius = radius_of(rad * ROWS + rows)
    gap = SPACING / radius
    step_log = minus_log(gap)
    next_log = minus_log(SPACING / radius_of(rad * ROWS + rows + 1))
    for c in range(CHUNKS):
        lanes = pl.ds(c * WIDE, WIDE)
        deg = degree_of(c * WIDE, WIDE)
        decay[:, lanes] = jnp.exp(-deg * next_log)
        rise[:, lanes] = jnp.exp(-deg * step_log) * (1.0 - gap)
        t = (2.0 * deg + 1.0) * step_log
        em = t * (1.0 - t * (1 / 2) * (1.0 - t * (1 / 3) * (1.0 - t * (1 / 4) * (1.0 - t * (1 / 5) * (1.0 - t * (1 / 6) * (1.0 - t * (1 / 7)))))))
        em = jnp.where(rows + (0 if c < OWN else rad * ROWS) == 0, 1.0, em)
        scale[:, lanes] = jnp.sqrt((16.0 * math.pi**2 / ANGLES) / (2.0 * deg + 1.0) * radius * em)

    for copy in loads[:2]:
        copy.wait()
    orb = orb_v[...]

    @pl.loop(0, FUNCS // 2)
    def _(pair):
        d = fn_v[pl.ds(2 * pair, 2)].astype(F32) * orb[None]
        dens[pl.ds(pl.multiple_of(pair * 80, 16), 80), :] = d.reshape(80, ANGLES).astype(BF16)

    loads[2].wait()

    lane = lax.broadcasted_iota(jnp.int32, (FUNCS, 128), 1)

    def put_tiles(c, first_row, k, ys, odd, spare):
        i = first_row + k
        if c < CHUNKS - 1:
            for h in range(2):
                y_buf[c, ROWS * h + i] = ys[h].astype(BF16)
            return odd, spare
        y_buf[c, i] = ys[0].astype(BF16)
        spare = jnp.where(lane == i, ys[1][:, 64:65], spare)
        if k % 2:
            y_buf[c, ROWS + first_row // 2 + k // 2] = jnp.where(lane < 64, odd, pltpu.roll(ys[1], 64, 1)).astype(BF16)
        return ys[1], spare

    def send_chunk(c):
        for peer in fn_peers:
            y_copy(c, peer, fn).start()
        y_in[c, fn, 0:TILES[c]] = y_buf[c, pl.ds(share(c, fn) * TILES[c], TILES[c])]

    for c in range(CHUNKS):
        width = min(WIDE, HARM - c * WIDE)
        out = lax.dot_general(
            dens[...], ylm_v[:, c * WIDE:c * WIDE + width], (((1,), (0,)), ((), ())), preferred_element_type=F32
        )
        if width == WIDE:
            proj[0] = out[:, :128]
            proj[1] = out[:, 128:]
        else:
            proj[0] = out[:, :128]
            proj[1] = jnp.zeros_like(proj[1])
            proj[1, :, 0:width - 128] = out[:, 128:]

        base = c * WIDE

        def back(step, n):
            first_row = pl.multiple_of(8 * (ROWS // 8 - 1 - step), 8)
            down = decay[pl.ds(first_row, 8), base:base + WIDE]
            up = scale[pl.ds(first_row, 8), base:base + WIDE]
            for k in reversed(range(8)):
                i = first_row + k
                r_i = 1.0 + SPACING * ((rad * ROWS + i).astype(F32) + 0.5)
                factor = SPACING * weight[i] * r_i
                new = []
                for h in range(2):
                    lanes = slice(128 * h, 128 * h + 128)
                    s = proj[h, pl.ds(i, FUNCS, stride=ROWS), :] * factor
                    src[2 * c + h, i] = s
                    v = s + down[k:k + 1, lanes] * n[h]
                    inw[2 * c + h, i] = v
                    new.append(v)
                if c < OWN:
                    put_tiles(c, first_row, k, [new[h] * up[k:k + 1, 128 * h:128 * h + 128] for h in range(2)], None, None)
                n = tuple(new)
            return n

        zero = jnp.zeros((FUNCS, 128), F32)
        first = lax.fori_loop(0, ROWS // 8, back, (zero, zero))
        for h in range(2):
            edge[1, :, base + 128 * h:base + 128 * h + 128] = first[h].astype(BF16)

        if c == 0:
            pl.semaphore_wait(barrier, len(FN_STEPS) + RADS - 1)
        if c < OWN:
            send_chunk(c)

        def forth(step, o):
            first_row = pl.multiple_of(8 * step, 8)
            up = rise[pl.ds(first_row, 8), base:base + WIDE]
            for k in range(8):
                o = tuple(
                    src[2 * c + h, first_row + k] + up[k:k + 1, 128 * h:128 * h + 128] * o[h] for h in range(2)
                )
            return o

        last = lax.fori_loop(0, ROWS // 8, forth, (zero, zero))
        for h in range(2):
            edge[0, :, base + 128 * h:base + 128 * h + 128] = last[h].astype(BF16)

    @pl.loop(1, RADS)
    def _(step):
        peer = lax.rem(rad + step, RADS)
        pltpu.make_async_remote_copy(
            src_ref=edge.at[jnp.where(peer > rad, 0, 1)],
            dst_ref=edge_in.at[rad],
            send_sem=e_send.at[peer],
            recv_sem=e_recv.at[rad],
            device_id=(peer, fn),
            device_id_type=MESH,
        ).start()

    edge_in[rad] = jnp.zeros((FUNCS, CHUNKS * WIDE), BF16)
    blocks = lax.broadcasted_iota(jnp.int32, (RADS, 1), 0)
    log_last = jnp.log(radius_of(blocks * ROWS + (ROWS - 1)))
    log_first = jnp.log(radius_of(blocks * ROWS))
    spot = jnp.full((1, 1), rad, jnp.int32)
    log_end = jnp.log(radius_of(spot * ROWS - 1))
    log_next = jnp.log(radius_of(spot * ROWS + ROWS))
    log_row = jnp.log(radius)
    for c in range(CHUNKS):
        lanes = pl.ds(c * WIDE, WIDE)
        deg = degree_of(c * WIDE, WIDE)
        couple_o[:, lanes] = jnp.where(blocks < spot, jnp.exp((deg + 1.0) * jnp.minimum(log_last - log_end, 0.0)), 0.0)
        couple_n[:, lanes] = jnp.where(blocks > spot, jnp.exp(deg * jnp.minimum(log_next - log_first, 0.0)), 0.0)
        fall[:, lanes] = jnp.exp(deg * jnp.minimum(log_row - log_next, 0.0))

    @pl.loop(1, RADS)
    def _(step):
        peer = lax.rem(rad + step, RADS)
        pltpu.make_async_remote_copy(
            src_ref=edge.at[0], dst_ref=edge_in.at[peer], send_sem=e_send.at[peer], recv_sem=e_recv.at[peer],
            device_id=(peer, fn), device_id_type=MESH,
        ).wait_recv()

    carries = []
    for t in range(2 * CHUNKS):
        lanes = slice(128 * t, 128 * t + 128)
        out_carry = jnp.zeros((FUNCS, 128), F32)
        in_carry = jnp.zeros((FUNCS, 128), F32)
        for b in range(RADS):
            e = edge_in[b, :, lanes].astype(F32)
            out_carry = out_carry + couple_o[b:b + 1, lanes] * e
            in_carry = in_carry + couple_n[b:b + 1, lanes] * e
        carries.append((out_carry, in_carry))
        if t < 2 * OWN:
            x_buf[t] = (out_carry * (scale[0:1, lanes] * rise[0:1, lanes])).astype(BF16)

    for c in range(OWN, CHUNKS):
        base = c * WIDE

        def whole(step, spare):
            first_row = pl.multiple_of(8 * step, 8)
            up = scale[pl.ds(first_row, 8), base:base + WIDE]
            far = fall[pl.ds(first_row, 8), base:base + WIDE]
            odd = None
            for k in range(8):
                ys = []
                for h in range(2):
                    lanes = slice(128 * h, 128 * h + 128)
                    v = inw[2 * c + h, first_row + k] + far[k:k + 1, lanes] * carries[2 * c + h][1]
                    ys.append(v * up[k:k + 1, lanes])
                odd, spare = put_tiles(c, first_row, k, ys, odd, spare)
            return spare

        spare = lax.fori_loop(0, ROWS // 8, whole, jnp.zeros((FUNCS, 128), F32))
        if c == CHUNKS - 1:
            y_buf[c, ROWS + ROWS // 2] = spare.astype(BF16)
            y_buf[c, ROWS + ROWS // 2 + 1:FNS * TILES[c]] = jnp.zeros((3, FUNCS, 128), BF16)
        send_chunk(c)
        if c == OWN:
            for t in range(2 * OWN):
                owner = first_owner(t // 2, t % 2)

                @pl.when(owner != fn)
                def _():
                    x_copy(t, owner, fn).start()

                @pl.when(owner == fn)
                def _():
                    x_in[fn] = x_buf[t]

    for t in range(2 * CHUNKS):
        lanes = slice(128 * t, 128 * t + 128)
        multipole = (4.0 * math.pi) / (2.0 * degree_of(128 * t, 128) + 1.0)
        out_carry, in_carry = carries[t]

        def forth(step, o):
            first_row = pl.multiple_of(8 * step, 8)
            up = rise[pl.ds(first_row, 8), lanes]
            far = fall[pl.ds(first_row, 8), lanes]
            for k in range(8):
                i = first_row + k
                grown = up[k:k + 1] * o
                total = grown + inw[t, i] + far[k:k + 1] * in_carry
                coef[t, pl.ds(i, FUNCS, stride=ROWS), :] = multipole * total
                o = grown + src[t, i]
            return o

        lax.fori_loop(0, ROWS // 8, forth, out_carry)

    @pl.loop(0, FUNCS // 4)
    def _(quad):
        at = pl.ds(pl.multiple_of(quad * 160, 16), 160)
        left = jnp.concatenate([coef[t, at, :].astype(BF16) for t in range(2 * CHUNKS)], axis=1)[:, :HARM]
        out = lax.dot_general(left, ylm_v[...], (((1,), (1,)), ((), ())), preferred_element_type=F32)
        potential[pl.ds(4 * quad, 4)] = out.reshape(4, ROWS, ANGLES).astype(BF16)

    @pl.loop(1, RADS)
    def _(step):
        peer = lax.rem(rad + step, RADS)
        pltpu.make_async_remote_copy(
            src_ref=edge.at[0], dst_ref=edge_in.at[rad], send_sem=e_send.at[peer], recv_sem=e_recv.at[rad],
            device_id=(peer, fn), device_id_type=MESH,
        ).wait_send()

    def gram_of(left, right):
        return lax.dot_general(left, right, (((1,), (1,)), ((), ())), preferred_element_type=F32)

    for c in range(CHUNKS):
        for peer in fn_peers:
            y_copy(c, peer, peer).wait_recv()
        x = jnp.concatenate([y_in[c, :, t].reshape(FNS * FUNCS, 128) for t in range(TILES[c])], axis=1)
        if c == 0:
            gram[...] = gram_of(x, x)
        elif c < CHUNKS - 1:
            gram[...] += gram_of(x, x)
        else:
            part[...] = (gram[...] + gram_of(x, x)).astype(BF16)
        if c == CHUNKS - 2:
            for t in range(2 * OWN):

                @pl.when(first_owner(t // 2, t % 2) == fn)
                def _():
                    for peer in fn_peers:
                        x_copy(t, peer, peer).wait_recv()
                    p = x_in[...].reshape(FNS * FUNCS, 128)
                    a = y_in[t // 2, :, 0].reshape(FNS * FUNCS, 128)
                    gram[...] += gram_of(a, p) + gram_of(p, a)

    def part_copy(peer, slot):
        return pltpu.make_async_remote_copy(
            src_ref=part.at[pl.ds(pl.multiple_of(peer * FUNCS, 16), FUNCS)], dst_ref=part_in.at[slot],
            send_sem=p_send.at[peer], recv_sem=p_recv.at[slot], device_id=(peer, fn), device_id_type=MESH,
        )

    rad_peers = [lax.rem(rad + step, RADS) for step in RAD_STEPS]
    for peer in rad_peers:
        part_copy(peer, rad).start()

    for c in range(CHUNKS):
        for peer in fn_peers:
            y_copy(c, peer, fn).wait_send()
    for t in range(2 * OWN):
        owner = first_owner(t // 2, t % 2)

        @pl.when(owner != fn)
        def _():
            x_copy(t, owner, fn).wait_send()


    total = part[pl.ds(pl.multiple_of(rad * FUNCS, 16), FUNCS), :].astype(F32)

    for peer in rad_peers:
        part_copy(peer, peer).wait_recv()
        total = total + part_in[peer].astype(F32)

    for h in range(2):
        for q in range(2):
            tile = swap_blocks(total[8 * h:8 * h + 8, 128 * q:128 * q + 128])
            for k in range(8):
                slab[8 * q + k, h:h + 1, :] = tile[k:k + 1, :]

    def slab_copy(peer, slot):
        return pltpu.make_async_remote_copy(
            src_ref=slab.at[peer], dst_ref=slab_in.at[slot], send_sem=s_send.at[peer],
            recv_sem=s_recv.at[slot], device_id=(rad, peer), device_id_type=MESH,
        )

    for peer in fn_peers:
        slab_copy(peer, fn).start()
    for peer in rad_peers:
        part_copy(peer, rad).wait_send()
    total = slab[fn]
    for peer in fn_peers:
        slab_copy(peer, peer).wait_recv()
        total = total + slab_in[peer]
    for h in range(2):
        tile = swap_blocks(jnp.broadcast_to(total[h:h + 1], (8, 128)))
        matrix[8 * h:8 * h + 8, :] = tile[:, :FUNCS]

    for peer in fn_peers:
        slab_copy(peer, fn).wait_send()


def local(functions, orbital, radial_weight, ylm):
    hbm = pl.BlockSpec(memory_space=pltpu.HBM)
    vmem, dma = pltpu.VMEM, pltpu.SemaphoreType.DMA
    lanes = CHUNKS * WIDE
    return pl.pallas_call(
        kernel,
        out_shape=(vmem((FUNCS, ROWS, ANGLES), BF16), vmem((FUNCS, FUNCS), F32)),
        in_specs=[hbm, hbm, pl.BlockSpec(memory_space=pltpu.SMEM), hbm],
        out_specs=(pl.BlockSpec(memory_space=pltpu.VMEM), pl.BlockSpec(memory_space=pltpu.VMEM)),
        scratch_shapes=[
            vmem((FUNCS, ROWS, ANGLES), BF16),
            vmem((ROWS, ANGLES), F32),
            vmem((ANGLES, HARM), BF16),
            vmem((FUNCS * ROWS, ANGLES), BF16),
            vmem((2, FUNCS * ROWS, 128), F32),
            vmem((2 * CHUNKS, ROWS, FUNCS, 128), F32),
            vmem((2 * CHUNKS, ROWS, FUNCS, 128), F32),
            vmem((2 * CHUNKS, FUNCS * ROWS, 128), F32),
            vmem((ROWS, lanes), F32),
            vmem((ROWS, lanes), F32),
            vmem((ROWS, lanes), F32),
            vmem((ROWS, lanes), F32),
            vmem((RADS, lanes), F32),
            vmem((RADS, lanes), F32),
            vmem((CHUNKS, 2 * ROWS, FUNCS, 128), BF16),
            vmem((CHUNKS, FNS, max(TILES), FUNCS, 128), BF16),
            vmem((2 * OWN, FUNCS, 128), BF16),
            vmem((FNS, FUNCS, 128), BF16),
            vmem((2, FUNCS, lanes), BF16),
            vmem((RADS, FUNCS, lanes), BF16),
            vmem((FNS * FUNCS, FNS * FUNCS), F32),
            vmem((FNS * FUNCS, FNS * FUNCS), BF16),
            vmem((RADS, FUNCS, FNS * FUNCS), BF16),
            vmem((FNS, 2, 128), F32),
            vmem((FNS, 2, 128), F32),
            dma((3,)),
            dma((CHUNKS, FNS)), dma((CHUNKS, FNS)),
            dma((2 * OWN,)), dma((FNS,)),
            dma((RADS,)), dma((RADS,)),
            dma((RADS,)), dma((RADS,)),
            dma((FNS,)), dma((FNS,)),
        ],
        compiler_params=pltpu.CompilerParams(
            collective_id=0, has_side_effects=True, vmem_limit_bytes=61 * 2**20
        ),
    )(functions, orbital, radial_weight, ylm.T)


def solution(mesh):
    in_specs = (P("fn", "rad", None), P("rad", None), P("rad"), P())
    out_specs = (P("fn", "rad", None), P("rad", "fn"))
    return jax.shard_map(local, mesh=mesh, in_specs=in_specs, out_specs=out_specs, check_vma=False)
```

```python
import functools
import math

import jax
import jax.numpy as jnp
from jax import lax
from jax.experimental import pallas as pl
from jax.experimental.pallas import tpu as pltpu
from jax.sharding import PartitionSpec as P

MESH = pl.DeviceIdType.MESH
F32, BF16 = jnp.float32, jnp.bfloat16
ANGLES, HARM, RADII = 1202, 961, 640
RADS, FNS = 16, 16
ROWS, FUNCS = 40, 16
SPACING = 3.0 / RADII
CHUNKS, WIDE = 4, 256
TILES = (5, 5, 5, 4)
OWN = 3
FN_STEPS = [(y, z) for z in (4, 3, 5, 2, 6, 1, 7, 0) for y in (0, 1) if (y, z) != (0, 0)]


def degree_of(first, width):
    m = first + lax.broadcasted_iota(jnp.int32, (1, width), 1)
    return jnp.floor(jnp.sqrt(m.astype(F32) + 0.5))


RAD_STEPS = (8, 7, 9, 6, 10, 5, 11, 4, 12, 3, 13, 2, 14, 1, 15)


def swap_blocks(x):
    row = lax.broadcasted_iota(jnp.int32, (8, 128), 0)
    block = lax.broadcasted_iota(jnp.int32, (8, 128), 1) // 16
    for b in (1, 2, 4):
        row_bit, block_bit = (row // b) % 2, (block // b) % 2
        above = pltpu.roll(pltpu.roll(x, 8 - b, 0), 16 * b, 1)
        below = pltpu.roll(pltpu.roll(x, b, 0), 128 - 16 * b, 1)
        x = jnp.where(row_bit == block_bit, x, jnp.where(block_bit == 1, above, below))
    return x


def kernel(
    functions, orbital, weight, ylm,
    potential, matrix,
    fn_v, orb_v, ylm_v, dens, proj, src, inw, coef,
    decay, rise, scale, fall, couple_o, couple_n,
    y_buf, y_in, x_buf, x_in, edge, edge_in, gram, part, part_in, slab, slab_in,
    load_sem, y_send, y_recv, x_send, x_recv, e_send, e_recv, p_send, p_recv, s_send, s_recv,
):
    rad, fn = lax.axis_index("rad"), lax.axis_index("fn")
    fn_y, fn_z = fn // 8, lax.rem(fn, 8)
    fn_peers = [lax.rem(fn_y + y, 2) * 8 + lax.rem(fn_z + z, 8) for y, z in FN_STEPS]

    loads = [
        pltpu.make_async_copy(functions, fn_v, load_sem.at[0]),
        pltpu.make_async_copy(orbital, orb_v, load_sem.at[1]),
        pltpu.make_async_copy(ylm, ylm_v, load_sem.at[2]),
    ]
    barrier = pltpu.get_barrier_semaphore()
    for peer in fn_peers:
        pl.semaphore_signal(barrier, inc=1, device_id=(rad, peer), device_id_type=MESH)

    @pl.loop(1, RADS)
    def _(step):
        pl.semaphore_signal(barrier, inc=1, device_id=(lax.rem(rad + step, RADS), fn), device_id_type=MESH)

    for copy in loads:
        copy.start()

    core = lax.rem(rad, 2)

    def share(c, peer):
        y, z = peer // 8, lax.rem(peer, 8)
        return y * 8 + lax.rem(z + 4 * y + 6 * core + 8 - c, 8)

    def first_owner(c, h):
        return h * 8 + lax.rem(4 * h + 2 * core + c, 8)

    def y_copy(c, peer, slot):
        return pltpu.make_async_remote_copy(
            src_ref=y_buf.at[c, pl.ds(share(c, peer) * TILES[c], TILES[c])], dst_ref=y_in.at[c, slot, pl.ds(0, TILES[c])],
            send_sem=y_send.at[c, peer], recv_sem=y_recv.at[c, slot], device_id=(rad, peer), device_id_type=MESH,
        )

    def x_copy(t, peer, slot):
        return pltpu.make_async_remote_copy(
            src_ref=x_buf.at[t], dst_ref=x_in.at[slot], send_sem=x_send.at[t], recv_sem=x_recv.at[slot],
            device_id=(rad, peer), device_id_type=MESH,
        )

    def radius_of(position):
        return 1.0 + SPACING * (position.astype(F32) + 0.5)

    def minus_log(x):
        return x * (1.0 + x * (0.5 + x * (1.0 / 3.0 + x * 0.25)))

    rows = lax.broadcasted_iota(jnp.int32, (ROWS, 1), 0)
    radius = radius_of(rad * ROWS + rows)
    gap = SPACING / radius
    step_log = minus_log(gap)
    next_log = minus_log(SPACING / radius_of(rad * ROWS + rows + 1))
    for c in range(CHUNKS):
        lanes = pl.ds(c * WIDE, WIDE)
        deg = degree_of(c * WIDE, WIDE)
        decay[:, lanes] = jnp.exp(-deg * next_log)
        rise[:, lanes] = jnp.exp(-deg * step_log) * (1.0 - gap)
        t = (2.0 * deg + 1.0) * step_log
        em = t * (1.0 - t * (1 / 2) * (1.0 - t * (1 / 3) * (1.0 - t * (1 / 4) * (1.0 - t * (1 / 5) * (1.0 - t * (1 / 6) * (1.0 - t * (1 / 7)))))))
        em = jnp.where(rows + (0 if c < OWN else rad * ROWS) == 0, 1.0, em)
        scale[:, lanes] = jnp.sqrt((16.0 * math.pi**2 / ANGLES) / (2.0 * deg + 1.0) * radius * em)

    for copy in loads[:2]:
        copy.wait()
    orb = orb_v[...]

    @pl.loop(0, FUNCS // 2)
    def _(pair):
        d = fn_v[pl.ds(2 * pair, 2)].astype(F32) * orb[None]
        dens[pl.ds(pl.multiple_of(pair * 80, 16), 80), :] = d.reshape(80, ANGLES).astype(BF16)

    loads[2].wait()

    lane = lax.broadcasted_iota(jnp.int32, (FUNCS, 128), 1)

    def put_tiles(c, first_row, k, ys, odd, spare):
        i = first_row + k
        if c < CHUNKS - 1:
            for h in range(2):
                y_buf[c, ROWS * h + i] = ys[h].astype(BF16)
            return odd, spare
        y_buf[c, i] = ys[0].astype(BF16)
        spare = jnp.where(lane == i, ys[1][:, 64:65], spare)
        if k % 2:
            y_buf[c, ROWS + first_row // 2 + k // 2] = jnp.where(lane < 64, odd, pltpu.roll(ys[1], 64, 1)).astype(BF16)
        return ys[1], spare

    def send_chunk(c):
        for peer in fn_peers:
            y_copy(c, peer, fn).start()
        y_in[c, fn, 0:TILES[c]] = y_buf[c, pl.ds(share(c, fn) * TILES[c], TILES[c])]

    for c in range(CHUNKS):
        width = min(WIDE, HARM - c * WIDE)
        out = lax.dot_general(
            dens[...], ylm_v[:, c * WIDE:c * WIDE + width], (((1,), (0,)), ((), ())), preferred_element_type=F32
        )
        if width == WIDE:
            proj[0] = out[:, :128]
            proj[1] = out[:, 128:]
        else:
            proj[0] = out[:, :128]
            proj[1] = jnp.zeros_like(proj[1])
            proj[1, :, 0:width - 128] = out[:, 128:]

        base = c * WIDE

        def back(step, n):
            first_row = pl.multiple_of(8 * (ROWS // 8 - 1 - step), 8)
            down = decay[pl.ds(first_row, 8), base:base + WIDE]
            up = scale[pl.ds(first_row, 8), base:base + WIDE]
            for k in reversed(range(8)):
                i = first_row + k
                r_i = 1.0 + SPACING * ((rad * ROWS + i).astype(F32) + 0.5)
                factor = SPACING * weight[i] * r_i
                new = []
                for h in range(2):
                    lanes = slice(128 * h, 128 * h + 128)
                    s = proj[h, pl.ds(i, FUNCS, stride=ROWS), :] * factor
                    src[2 * c + h, i] = s
                    v = s + down[k:k + 1, lanes] * n[h]
                    inw[2 * c + h, i] = v
                    new.append(v)
                if c < OWN:
                    put_tiles(c, first_row, k, [new[h] * up[k:k + 1, 128 * h:128 * h + 128] for h in range(2)], None, None)
                n = tuple(new)
            return n

        zero = jnp.zeros((FUNCS, 128), F32)
        first = lax.fori_loop(0, ROWS // 8, back, (zero, zero))
        for h in range(2):
            edge[1, :, base + 128 * h:base + 128 * h + 128] = first[h].astype(BF16)

        if c == 0:
            pl.semaphore_wait(barrier, len(FN_STEPS) + RADS - 1)
        if c < OWN:
            send_chunk(c)

        def forth(step, o):
            first_row = pl.multiple_of(8 * step, 8)
            up = rise[pl.ds(first_row, 8), base:base + WIDE]
            for k in range(8):
                o = tuple(
                    src[2 * c + h, first_row + k] + up[k:k + 1, 128 * h:128 * h + 128] * o[h] for h in range(2)
                )
            return o

        last = lax.fori_loop(0, ROWS // 8, forth, (zero, zero))
        for h in range(2):
            edge[0, :, base + 128 * h:base + 128 * h + 128] = last[h].astype(BF16)

    @pl.loop(1, RADS)
    def _(step):
        peer = lax.rem(rad + step, RADS)
        pltpu.make_async_remote_copy(
            src_ref=edge.at[jnp.where(peer > rad, 0, 1)],
            dst_ref=edge_in.at[rad],
            send_sem=e_send.at[peer],
            recv_sem=e_recv.at[rad],
            device_id=(peer, fn),
            device_id_type=MESH,
        ).start()

    edge_in[rad] = jnp.zeros((FUNCS, CHUNKS * WIDE), BF16)
    blocks = lax.broadcasted_iota(jnp.int32, (RADS, 1), 0)
    log_last = jnp.log(radius_of(blocks * ROWS + (ROWS - 1)))
    log_first = jnp.log(radius_of(blocks * ROWS))
    spot = jnp.full((1, 1), rad, jnp.int32)
    log_end = jnp.log(radius_of(spot * ROWS - 1))
    log_next = jnp.log(radius_of(spot * ROWS + ROWS))
    log_row = jnp.log(radius)
    for c in range(CHUNKS):
        lanes = pl.ds(c * WIDE, WIDE)
        deg = degree_of(c * WIDE, WIDE)
        couple_o[:, lanes] = jnp.where(blocks < spot, jnp.exp((deg + 1.0) * jnp.minimum(log_last - log_end, 0.0)), 0.0)
        couple_n[:, lanes] = jnp.where(blocks > spot, jnp.exp(deg * jnp.minimum(log_next - log_first, 0.0)), 0.0)
        fall[:, lanes] = jnp.exp(deg * jnp.minimum(log_row - log_next, 0.0))

    @pl.loop(1, RADS)
    def _(step):
        peer = lax.rem(rad + step, RADS)
        pltpu.make_async_remote_copy(
            src_ref=edge.at[0], dst_ref=edge_in.at[peer], send_sem=e_send.at[peer], recv_sem=e_recv.at[peer],
            device_id=(peer, fn), device_id_type=MESH,
        ).wait_recv()

    carries = []
    for t in range(2 * CHUNKS):
        lanes = slice(128 * t, 128 * t + 128)
        out_carry = jnp.zeros((FUNCS, 128), F32)
        in_carry = jnp.zeros((FUNCS, 128), F32)
        for b in range(RADS):
            e = edge_in[b, :, lanes].astype(F32)
            out_carry = out_carry + couple_o[b:b + 1, lanes] * e
            in_carry = in_carry + couple_n[b:b + 1, lanes] * e
        carries.append((out_carry, in_carry))
        if t < 2 * OWN:
            x_buf[t] = (out_carry * (scale[0:1, lanes] * rise[0:1, lanes])).astype(BF16)

    for c in range(OWN, CHUNKS):
        base = c * WIDE

        def whole(step, spare):
            first_row = pl.multiple_of(8 * step, 8)
            up = scale[pl.ds(first_row, 8), base:base + WIDE]
            far = fall[pl.ds(first_row, 8), base:base + WIDE]
            odd = None
            for k in range(8):
                ys = []
                for h in range(2):
                    lanes = slice(128 * h, 128 * h + 128)
                    v = inw[2 * c + h, first_row + k] + far[k:k + 1, lanes] * carries[2 * c + h][1]
                    ys.append(v * up[k:k + 1, lanes])
                odd, spare = put_tiles(c, first_row, k, ys, odd, spare)
            return spare

        spare = lax.fori_loop(0, ROWS // 8, whole, jnp.zeros((FUNCS, 128), F32))
        if c == CHUNKS - 1:
            y_buf[c, ROWS + ROWS // 2] = spare.astype(BF16)
            y_buf[c, ROWS + ROWS // 2 + 1:FNS * TILES[c]] = jnp.zeros((3, FUNCS, 128), BF16)
        send_chunk(c)
        if c == OWN:
            for t in range(2 * OWN):
                owner = first_owner(t // 2, t % 2)

                @pl.when(owner != fn)
                def _():
                    x_copy(t, owner, fn).start()

                @pl.when(owner == fn)
                def _():
                    x_in[fn] = x_buf[t]

    for t in range(2 * CHUNKS):
        lanes = slice(128 * t, 128 * t + 128)
        multipole = (4.0 * math.pi) / (2.0 * degree_of(128 * t, 128) + 1.0)
        out_carry, in_carry = carries[t]

        def forth(step, o):
            first_row = pl.multiple_of(8 * step, 8)
            up = rise[pl.ds(first_row, 8), lanes]
            far = fall[pl.ds(first_row, 8), lanes]
            for k in range(8):
                i = first_row + k
                grown = up[k:k + 1] * o
                total = grown + inw[t, i] + far[k:k + 1] * in_carry
                coef[t, pl.ds(i, FUNCS, stride=ROWS), :] = multipole * total
                o = grown + src[t, i]
            return o

        lax.fori_loop(0, ROWS // 8, forth, out_carry)

    @pl.loop(0, FUNCS // 4)
    def _(quad):
        at = pl.ds(pl.multiple_of(quad * 160, 16), 160)
        left = jnp.concatenate([coef[t, at, :].astype(BF16) for t in range(2 * CHUNKS)], axis=1)[:, :HARM]
        out = lax.dot_general(left, ylm_v[...], (((1,), (1,)), ((), ())), preferred_element_type=F32)
        potential[pl.ds(4 * quad, 4)] = out.reshape(4, ROWS, ANGLES).astype(BF16)

    @pl.loop(1, RADS)
    def _(step):
        peer = lax.rem(rad + step, RADS)
        pltpu.make_async_remote_copy(
            src_ref=edge.at[0], dst_ref=edge_in.at[rad], send_sem=e_send.at[peer], recv_sem=e_recv.at[rad],
            device_id=(peer, fn), device_id_type=MESH,
        ).wait_send()

    def gram_of(left, right):
        return lax.dot_general(left, right, (((1,), (1,)), ((), ())), preferred_element_type=F32)

    for c in range(CHUNKS):
        if c > 0:
            for peer in fn_peers:
                y_copy(c - 1, peer, fn).wait_send()
        for peer in fn_peers:
            y_copy(c, peer, peer).wait_recv()
        x = jnp.concatenate([y_in[c, :, t].reshape(FNS * FUNCS, 128) for t in range(TILES[c])], axis=1)
        if c == 0:
            gram[...] = gram_of(x, x)
        elif c < CHUNKS - 1:
            gram[...] += gram_of(x, x)
        else:
            part[...] = (gram[...] + gram_of(x, x)).astype(BF16)
        if c == CHUNKS - 2:
            for t in range(2 * OWN):

                @pl.when(first_owner(t // 2, t % 2) == fn)
                def _():
                    for peer in fn_peers:
                        x_copy(t, peer, peer).wait_recv()
                    p = x_in[...].reshape(FNS * FUNCS, 128)
                    a = y_in[t // 2, :, 0].reshape(FNS * FUNCS, 128)
                    gram[...] += gram_of(a, p) + gram_of(p, a)

    def part_copy(peer, slot):
        return pltpu.make_async_remote_copy(
            src_ref=part.at[pl.ds(pl.multiple_of(peer * FUNCS, 16), FUNCS)], dst_ref=part_in.at[slot],
            send_sem=p_send.at[peer], recv_sem=p_recv.at[slot], device_id=(peer, fn), device_id_type=MESH,
        )

    rad_peers = [lax.rem(rad + step, RADS) for step in RAD_STEPS]
    for peer in rad_peers:
        part_copy(peer, rad).start()

    for peer in fn_peers:
        y_copy(CHUNKS - 1, peer, fn).wait_send()
    for t in range(2 * OWN):
        owner = first_owner(t // 2, t % 2)

        @pl.when(owner != fn)
        def _():
            x_copy(t, owner, fn).wait_send()


    total = part[pl.ds(pl.multiple_of(rad * FUNCS, 16), FUNCS), :].astype(F32)

    for peer in rad_peers:
        part_copy(peer, peer).wait_recv()
        total = total + part_in[peer].astype(F32)

    for h in range(2):
        for q in range(2):
            tile = swap_blocks(total[8 * h:8 * h + 8, 128 * q:128 * q + 128])
            for k in range(8):
                slab[8 * q + k, h:h + 1, :] = tile[k:k + 1, :]

    def slab_copy(peer, slot):
        return pltpu.make_async_remote_copy(
            src_ref=slab.at[peer], dst_ref=slab_in.at[slot], send_sem=s_send.at[peer],
            recv_sem=s_recv.at[slot], device_id=(rad, peer), device_id_type=MESH,
        )

    for peer in fn_peers:
        slab_copy(peer, fn).start()
    for peer in rad_peers:
        part_copy(peer, rad).wait_send()
    total = slab[fn]
    for peer in fn_peers:
        slab_copy(peer, peer).wait_recv()
        total = total + slab_in[peer]
    for h in range(2):
        tile = swap_blocks(jnp.broadcast_to(total[h:h + 1], (8, 128)))
        matrix[8 * h:8 * h + 8, :] = tile[:, :FUNCS]

    for peer in fn_peers:
        slab_copy(peer, fn).wait_send()


def local(functions, orbital, radial_weight, ylm):
    hbm = pl.BlockSpec(memory_space=pltpu.HBM)
    vmem, dma = pltpu.VMEM, pltpu.SemaphoreType.DMA
    lanes = CHUNKS * WIDE
    return pl.pallas_call(
        kernel,
        out_shape=(vmem((FUNCS, ROWS, ANGLES), BF16), vmem((FUNCS, FUNCS), F32)),
        in_specs=[hbm, hbm, pl.BlockSpec(memory_space=pltpu.SMEM), hbm],
        out_specs=(pl.BlockSpec(memory_space=pltpu.VMEM), pl.BlockSpec(memory_space=pltpu.VMEM)),
        scratch_shapes=[
            vmem((FUNCS, ROWS, ANGLES), BF16),
            vmem((ROWS, ANGLES), F32),
            vmem((ANGLES, HARM), BF16),
            vmem((FUNCS * ROWS, ANGLES), BF16),
            vmem((2, FUNCS * ROWS, 128), F32),
            vmem((2 * CHUNKS, ROWS, FUNCS, 128), F32),
            vmem((2 * CHUNKS, ROWS, FUNCS, 128), F32),
            vmem((2 * CHUNKS, FUNCS * ROWS, 128), F32),
            vmem((ROWS, lanes), F32),
            vmem((ROWS, lanes), F32),
            vmem((ROWS, lanes), F32),
            vmem((ROWS, lanes), F32),
            vmem((RADS, lanes), F32),
            vmem((RADS, lanes), F32),
            vmem((CHUNKS, 2 * ROWS, FUNCS, 128), BF16),
            vmem((CHUNKS, FNS, max(TILES), FUNCS, 128), BF16),
            vmem((2 * OWN, FUNCS, 128), BF16),
            vmem((FNS, FUNCS, 128), BF16),
            vmem((2, FUNCS, lanes), BF16),
            vmem((RADS, FUNCS, lanes), BF16),
            vmem((FNS * FUNCS, FNS * FUNCS), F32),
            vmem((FNS * FUNCS, FNS * FUNCS), BF16),
            vmem((RADS, FUNCS, FNS * FUNCS), BF16),
            vmem((FNS, 2, 128), F32),
            vmem((FNS, 2, 128), F32),
            dma((3,)),
            dma((CHUNKS, FNS)), dma((CHUNKS, FNS)),
            dma((2 * OWN,)), dma((FNS,)),
            dma((RADS,)), dma((RADS,)),
            dma((RADS,)), dma((RADS,)),
            dma((FNS,)), dma((FNS,)),
        ],
        compiler_params=pltpu.CompilerParams(
            collective_id=0, has_side_effects=True, vmem_limit_bytes=61 * 2**20
        ),
    )(functions, orbital, radial_weight, ylm.T)


def solution(mesh):
    in_specs = (P("fn", "rad", None), P("rad", None), P("rad"), P())
    out_specs = (P("fn", "rad", None), P("rad", "fn"))
    return jax.shard_map(local, mesh=mesh, in_specs=in_specs, out_specs=out_specs, check_vma=False)
```
